256 devices in a mesh: ctx: 32 (over z_hi, y, core), tp: 8 (over x, z_lo).
Axes of the slice: x: 4, y: 4, z: 8 (z_hi: 4, z_lo: 2; z = z_hi * 2 + z_lo), core: 2. Of those that a mesh axis runs over, the one named last changes fastest.
Arguments:
- query_proj: bfloat16 [8192, 8192], P('ctx', 'tp'), may hold values from -6 to 6
- key_proj: bfloat16 [8192, 8192], P('ctx', 'tp'), may hold values from -6 to 6
- value_proj: bfloat16 [8192, 8192], P('ctx', 'tp'), may hold values from -6 to 6
- cotangent: bfloat16 [8192, 8192], P('ctx', 'tp'), may hold values from -6 to 6
- filter_taps: bfloat16 [8192, 8192], P(('ctx', 'tp')), may hold values from -94.552125 to 94.552125
Outputs:
- block_output: bfloat16 [8192, 8192], P('ctx', 'tp')
- grad_query: bfloat16 [8192, 8192], P('ctx', 'tp')
- grad_key: bfloat16 [8192, 8192], P('ctx', 'tp')
- grad_value: bfloat16 [8192, 8192], P('ctx', 'tp')
- grad_filter: bfloat16 [8192, 8192], P(('ctx', 'tp'))
The draws below stay inside these ranges and needn't reach their ends.
All inputs are finite; a program needn't handle non-finite values.
Results may differ from the reference program's by a relative error of at most 0.0058.
Values may be sent and summed in bfloat16 or wider, within the bound.
No kernel may reach another device: no remote copies, remote signals or barrier semaphores. Data moves between devices by JAX's collectives and lax.ppermute only.
A program may use at most 128 MiB of HBM per device.

```python
import math
import jax
import jax.numpy as jnp
from jax import lax

D = 8192
SEQ = 8192


def draw_filter_taps(key, part):
    key = jax.random.fold_in(key, 7)
    rate_key, noise_key = jax.random.split(key)
    slowest = math.log(0.1 / SEQ)
    fastest = math.log(1.0 / 30.0)
    noise = jax.random.truncated_normal(noise_key, -4.0, 4.0, (SEQ, D), jnp.float32)
    rates = jnp.exp(jax.random.uniform(rate_key, (1, D), jnp.float32, slowest, fastest))
    position = jnp.arange(SEQ, dtype=jnp.float32)[:, None]
    taps = noise * jnp.sqrt(2.0 * SEQ * rates) * jnp.exp(-rates * position)
    return taps.astype(jnp.bfloat16)


def level_of(own_key, shape, cuts, low, top_value):
    factor_of, own = 1.0, jax.random.fold_in(own_key, 6)
    for dim, shards_of in cuts:
        draws = jnp.exp(jax.random.uniform(jax.random.fold_in(own, dim), (shards_of,), jnp.float32, low / len(cuts), top_value / len(cuts)))
        factor_of = factor_of * jnp.repeat(draws, shape[dim] // shards_of).reshape([-1 if axis == dim else 1 for axis in range(len(shape))])
    return factor_of


def centred(own_key, extent, deviation, reach, shards=(), kind=jnp.bfloat16):
    values = deviation * jax.random.normal(own_key, extent, jnp.float32)
    if shards:
        values = values * level_of(own_key, extent, shards, -0.22, 0.18)
    return jnp.clip(values, -reach, reach).astype(kind)


def setup_inputs(seed: int = 0) -> dict:
    keys = jax.random.split(jax.random.key(seed), 6)
    query_proj = centred(keys[0], (SEQ, D), 1.0, 6.0, ((0, 32), (1, 8)))
    key_proj = centred(keys[1], (SEQ, D), 1.0, 6.0, ((0, 32), (1, 8)))
    value_proj = centred(keys[2], (SEQ, D), 1.0, 6.0, ((0, 32), (1, 8)))
    cotangent = centred(keys[3], (SEQ, D), 1.0, 6.0, ((0, 32), (1, 8)))
    filter_taps = draw_filter_taps(jax.random.fold_in(keys[5], 71), 0)
    return {"query_proj": query_proj, "key_proj": key_proj, "value_proj": value_proj, "cotangent": cotangent, "filter_taps": filter_taps}


def reference(query_proj, key_proj, value_proj, cotangent, filter_taps):
    gated_input = (key_proj.astype(jnp.float32) * value_proj.astype(jnp.float32)).astype(jnp.bfloat16)
    gate_grad = (cotangent.astype(jnp.float32) * query_proj.astype(jnp.float32)).astype(jnp.bfloat16)
    block_width = min(D, 256)
    padded_length = 2 * SEQ
    scale = SEQ ** -0.5

    def per_block(block_start):
        def column_slice(source):
            return lax.dynamic_slice_in_dim(source, block_start, block_width, 1).astype(jnp.float32)

        spec_input = jnp.fft.rfft(column_slice(gated_input), n=padded_length, axis=0)
        spec_grad = jnp.fft.rfft(column_slice(gate_grad), n=padded_length, axis=0)
        spec_filter = jnp.fft.rfft(column_slice(filter_taps), n=padded_length, axis=0)
        convolved = jnp.fft.irfft(spec_filter * spec_input, n=padded_length, axis=0)[:SEQ]
        adjoint = jnp.fft.irfft(jnp.conj(spec_filter) * spec_grad, n=padded_length, axis=0)[:SEQ]
        filter_grad = jnp.fft.irfft(spec_grad * jnp.conj(spec_input), n=padded_length, axis=0)[:SEQ]
        return ((scale * convolved).astype(jnp.bfloat16), (scale * adjoint).astype(jnp.bfloat16),
                (scale * filter_grad).astype(jnp.bfloat16))

    starts = jnp.arange(D // block_width, dtype=jnp.int32) * block_width
    pieces = lax.map(per_block, starts.astype(jnp.int32))

    def unblock(stacked):
        return jnp.transpose(stacked, (1, 0, 2)).reshape(SEQ, D)

    convolved = unblock(pieces[0])
    adjoint = unblock(pieces[1])
    grad_filter = unblock(pieces[2])
    convolved, adjoint = lax.optimization_barrier((convolved, adjoint))
    wide_conv = convolved.astype(jnp.float32)
    wide_adjoint = adjoint.astype(jnp.float32)
    block_output = (query_proj.astype(jnp.float32) * wide_conv).astype(jnp.bfloat16)
    grad_query = (cotangent.astype(jnp.float32) * wide_conv).astype(jnp.bfloat16)
    grad_key = (wide_adjoint * value_proj.astype(jnp.float32)).astype(jnp.bfloat16)
    grad_value = (wide_adjoint * key_proj.astype(jnp.float32)).astype(jnp.bfloat16)
    return block_output, grad_query, grad_key, grad_value, grad_filter
```

```python
import functools
import math

import jax
import jax.numpy as jnp
import ml_dtypes
import numpy as np
from jax import lax
from jax.experimental import pallas as pl
from jax.experimental.pallas import tpu as pltpu
from jax.sharding import PartitionSpec as P

F32 = jnp.float32
BF16 = jnp.bfloat16
LANES = 128
KEPT = 72
MIB = 1 << 20


def split_table(table):
    high = table.astype(ml_dtypes.bfloat16)
    low = (table - high.astype(np.float64)).astype(ml_dtypes.bfloat16)
    return high, low


def make_tables(seq_len):
    radix = 2 * seq_len // LANES
    blocks = radix // 2
    total = 2 * seq_len
    kept = radix // 2 + 1
    order = np.concatenate([np.arange(0, blocks, 2), np.arange(1, blocks, 2)])
    k1 = np.arange(KEPT)
    live = (k1 < kept).astype(np.float64)
    turn = 2 * math.pi * np.outer(k1, order) / radix
    first = np.concatenate([np.cos(turn) * live[:, None], -np.sin(turn) * live[:, None]], 0)
    first_table = np.concatenate(split_table(first), 1)
    lane = np.arange(LANES)
    twist = 2 * math.pi * np.outer(k1, lane) / total
    twist_real = np.tile(np.cos(twist), (1, 2)).astype(np.float32)
    twist_imag = np.tile(-np.sin(twist), (1, 2)).astype(np.float32)
    inner = 2 * math.pi * np.outer(lane, lane) / LANES
    cos, sin = np.cos(inner), np.sin(inner)
    ahead = split_table(np.block([[cos, -sin], [sin, cos]]))
    ahead_table = np.concatenate([ahead[0], ahead[0], ahead[1]], 0)
    back = split_table(np.block([[cos, sin], [-sin, cos]]))
    back_table = np.concatenate([back[0], back[0], back[1]], 0)
    weight = np.where((k1 == 0) | (k1 == radix // 2), 1.0, 2.0) * live
    weight = weight * seq_len ** (-0.5) / total
    last = split_table(np.concatenate([np.cos(turn.T) * weight, -np.sin(turn.T) * weight], 1))
    last_table = np.concatenate([last[0], last[0], last[1]], 1)
    return first_table, twist_real, twist_imag, ahead_table, back_table, last_table


def split_value(value):
    high = value.astype(BF16)
    low = (value - high.astype(F32)).astype(BF16)
    return high, low


def gather_kernel(query, key, value, cotangent, taps, out):
    width = query.shape[1]
    groups, rows, positions = out.shape
    lanes = rows // 3

    def place(start, array):
        turned = array.T.astype(BF16)
        out[:, start : start + lanes, :] = turned.reshape(groups, lanes, positions)

    place(0, key[...].astype(F32) * value[...].astype(F32))
    place(lanes, cotangent[...].astype(F32) * query[...].astype(F32))
    place(2 * lanes, taps[...].astype(F32))


def scatter_kernel(
    query, key, value, cotangent, back, block_output, grad_query, grad_key, grad_value, grad_filter
):
    groups, rows, positions = back.shape
    lanes = rows // 3

    def take(start):
        wide = back[:, start : start + lanes, :].astype(F32)
        return wide.reshape(groups * lanes, positions).T

    convolved = take(0)
    block_output[...] = (query[...].astype(F32) * convolved).astype(BF16)
    grad_query[...] = (cotangent[...].astype(F32) * convolved).astype(BF16)
    adjoint = take(lanes)
    grad_key[...] = (adjoint * value[...].astype(F32)).astype(BF16)
    grad_value[...] = (adjoint * key[...].astype(F32)).astype(BF16)
    grad_filter[...] = take(2 * lanes).astype(BF16)


def long_kernel(
    received, first, twist_real, twist_imag, ahead, back, last, out, even, odd, stage, spec_x, spec_g, spec_h
):
    sources, rows, positions = received.shape
    lanes = rows // 3
    chunk = 4

    def spectrum(start, spec):
        whole = received[:, start : start + lanes, :].astype(F32).reshape(sources * lanes, positions)
        even[...] = whole[:, :LANES]
        odd[...] = whole[:, LANES:]

        @pl.loop(0, lanes // 2)
        def _(pair):
            one = pl.ds(2 * pair, sources, stride=lanes)
            two = pl.ds(2 * pair + 1, sources, stride=lanes)
            both = jnp.concatenate(
                [
                    jnp.concatenate([even[one, :], even[two, :]], 1),
                    jnp.concatenate([odd[one, :], odd[two, :]], 1),
                ],
                0,
            ).astype(BF16)
            turned = jnp.dot(
                first[...], jnp.concatenate([both, both], 0), preferred_element_type=F32
            )
            real, imag = turned[:KEPT], turned[KEPT:]
            new_real = real * twist_real[...] - imag * twist_imag[...]
            new_imag = imag * twist_real[...] + real * twist_imag[...]
            at = pl.multiple_of(pair * 2 * KEPT, 2 * KEPT)
            stage[pl.ds(at, KEPT), :LANES] = new_real[:, :LANES]
            stage[pl.ds(at, KEPT), LANES:] = new_imag[:, :LANES]
            stage[pl.ds(at + KEPT, KEPT), :LANES] = new_real[:, LANES:]
            stage[pl.ds(at + KEPT, KEPT), LANES:] = new_imag[:, LANES:]

        @pl.loop(0, lanes // chunk)
        def _(step):
            at = pl.ds(pl.multiple_of(step * chunk * KEPT, chunk * KEPT), chunk * KEPT)
            high, low = split_value(stage[at, :])
            spec[at, :] = jnp.dot(
                jnp.concatenate([high, low, high], 1), ahead[...], preferred_element_type=F32
            )

    def finish(start, left, right, sign):
        @pl.loop(0, lanes // chunk)
        def _(step):
            at = pl.ds(pl.multiple_of(step * chunk * KEPT, chunk * KEPT), chunk * KEPT)
            left_real, left_imag = left[at, :LANES], left[at, LANES:]
            right_real, right_imag = right[at, :LANES], sign * right[at, LANES:]
            real = left_real * right_real - left_imag * right_imag
            imag = left_real * right_imag + left_imag * right_real
            high, low = split_value(jnp.concatenate([real, imag], 1))
            turned = jnp.dot(
                jnp.concatenate([high, low, high], 1), back[...], preferred_element_type=F32
            )
            for one in range(chunk):
                real = turned[one * KEPT : (one + 1) * KEPT, :LANES]
                imag = turned[one * KEPT : (one + 1) * KEPT, LANES:]
                cos, sin = twist_real[:, :LANES], twist_imag[:, :LANES]
                row = pl.ds(pl.multiple_of((step * chunk + one) * KEPT, KEPT), KEPT)
                stage[row, :LANES] = real * cos + imag * sin
                stage[row, LANES:] = imag * cos - real * sin

        @pl.loop(0, lanes // 2)
        def _(pair):
            at = pl.multiple_of(pair * 2 * KEPT, 2 * KEPT)
            one = stage[pl.ds(at, KEPT), :]
            two = stage[pl.ds(at + KEPT, KEPT), :]
            both = jnp.concatenate(
                [
                    jnp.concatenate([one[:, :LANES], two[:, :LANES]], 1),
                    jnp.concatenate([one[:, LANES:], two[:, LANES:]], 1),
                ],
                0,
            )
            high, low = split_value(both)
            signal = jnp.dot(
                last[...], jnp.concatenate([high, low, high], 0), preferred_element_type=F32
            )
            for which in range(2):
                row = pl.ds(2 * pair + which, sources, stride=lanes)
                half = signal[:, which * LANES : (which + 1) * LANES]
                even[row, :] = half[:sources]
                odd[row, :] = half[sources:]

        whole = jnp.concatenate([even[...], odd[...]], 1).astype(BF16)
        out[:, start : start + lanes, :] = whole.reshape(sources, lanes, positions)

    spectrum(0, spec_x)
    spectrum(lanes, spec_g)
    spectrum(2 * lanes, spec_h)
    finish(0, spec_h, spec_x, 1.0)
    finish(lanes, spec_g, spec_h, -1.0)
    finish(2 * lanes, spec_g, spec_x, -1.0)


def gather(query, key, value, cotangent, taps, ranks):
    positions, width = query.shape
    lanes = width // ranks
    groups = LANES // lanes
    column = pl.BlockSpec((positions, LANES), lambda i: (0, i))
    return pl.pallas_call(
        gather_kernel,
        grid=(width // LANES,),
        in_specs=[column] * 5,
        out_specs=pl.BlockSpec((groups, 3 * lanes, positions), lambda i: (i, 0, 0)),
        out_shape=jax.ShapeDtypeStruct((ranks, 3 * lanes, positions), BF16),
        compiler_params=pltpu.CompilerParams(vmem_limit_bytes=24 * MIB),
        cost_estimate=pl.CostEstimate(flops=10**6, bytes_accessed=4 * MIB, transcendentals=0),
    )(query, key, value, cotangent, taps)


def scatter(query, key, value, cotangent, back):
    positions, width = query.shape
    ranks, rows, _ = back.shape
    groups = LANES // (width // ranks)
    column = pl.BlockSpec((positions, LANES), lambda i: (0, i))
    return pl.pallas_call(
        scatter_kernel,
        grid=(width // LANES,),
        in_specs=[column] * 4 + [pl.BlockSpec((groups, rows, positions), lambda i: (i, 0, 0))],
        out_specs=[column] * 5,
        out_shape=[jax.ShapeDtypeStruct((positions, width), BF16)] * 5,
        compiler_params=pltpu.CompilerParams(vmem_limit_bytes=24 * MIB),
        cost_estimate=pl.CostEstimate(flops=10**6, bytes_accessed=6 * MIB, transcendentals=0),
    )(query, key, value, cotangent, back)


def long_convolution(received):
    sources, rows, positions = received.shape
    lanes = rows // 3
    tables = [jnp.asarray(table) for table in make_tables(sources * positions)]
    spectra = pltpu.VMEM((lanes * KEPT, 2 * LANES), F32)
    return pl.pallas_call(
        long_kernel,
        out_shape=jax.ShapeDtypeStruct(received.shape, BF16),
        scratch_shapes=[pltpu.VMEM((sources * lanes, LANES), F32)] * 2 + [spectra] * 4,
        compiler_params=pltpu.CompilerParams(vmem_limit_bytes=48 * MIB),
        cost_estimate=pl.CostEstimate(flops=10**10, bytes_accessed=3 * MIB, transcendentals=0),
    )(received, *tables)


def local(query_proj, key_proj, value_proj, cotangent, filter_taps):
    ranks = lax.axis_size("ctx")
    taps = lax.all_to_all(filter_taps, "tp", split_axis=1, concat_axis=0, tiled=True)
    sent = gather(query_proj, key_proj, value_proj, cotangent, taps, ranks)
    received = lax.all_to_all(sent, "ctx", split_axis=0, concat_axis=0, tiled=True)
    made = long_convolution(received)
    back = lax.all_to_all(made, "ctx", split_axis=0, concat_axis=0, tiled=True)
    outputs = scatter(query_proj, key_proj, value_proj, cotangent, back)
    grad_filter = lax.all_to_all(outputs[4], "tp", split_axis=0, concat_axis=1, tiled=True)
    return (*outputs[:4], grad_filter)


def solution(mesh):
    placed = (P("ctx", "tp"),) * 4 + (P(("ctx", "tp"), None),)
    return jax.shard_map(local, mesh=mesh, in_specs=placed, out_specs=placed, check_vma=False)
```

```python
import functools
import math

import jax
import jax.numpy as jnp
import ml_dtypes
import numpy as np
from jax import lax
from jax.experimental import pallas as pl
from jax.experimental.pallas import tpu as pltpu
from jax.sharding import PartitionSpec as P

F32 = jnp.float32
BF16 = jnp.bfloat16
LANES = 128
KEPT = 72
MIB = 1 << 20
CHUNK = 4


def split_table(table):
    high = table.astype(ml_dtypes.bfloat16)
    low = (table - high.astype(np.float64)).astype(ml_dtypes.bfloat16)
    return high, low


def make_tables(seq_len):
    radix = 2 * seq_len // LANES
    blocks = radix // 2
    total = 2 * seq_len
    kept = radix // 2 + 1
    order = np.concatenate([np.arange(0, blocks, 2), np.arange(1, blocks, 2)])
    k1 = np.arange(KEPT)
    live = (k1 < kept).astype(np.float64)
    turn = 2 * math.pi * np.outer(k1, order) / radix
    first = np.concatenate([np.cos(turn) * live[:, None], -np.sin(turn) * live[:, None]], 0)
    first_table = np.concatenate(split_table(first), 1)
    lane = np.arange(LANES)
    twist = 2 * math.pi * np.outer(k1, lane) / total
    twist_real = np.tile(np.cos(twist), (1, 2)).astype(np.float32)
    twist_imag = np.tile(-np.sin(twist), (1, 2)).astype(np.float32)
    inner = 2 * math.pi * np.outer(lane, lane) / LANES
    cos, sin = np.cos(inner), np.sin(inner)
    ahead = split_table(np.block([[cos, -sin], [sin, cos]]))
    ahead_table = np.concatenate([ahead[0], ahead[0], ahead[1]], 0)
    back = split_table(np.block([[cos, sin], [-sin, cos]]))
    back_table = np.concatenate([back[0], back[0], back[1]], 0)
    weight = np.where((k1 == 0) | (k1 == radix // 2), 1.0, 2.0) * live
    weight = weight * seq_len ** (-0.5) / total
    last = split_table(np.concatenate([np.cos(turn.T) * weight, -np.sin(turn.T) * weight], 1))
    last_table = np.concatenate([last[0], last[0], last[1]], 1)
    return first_table, twist_real, twist_imag, ahead_table, back_table, last_table


def split_value(value):
    high = value.astype(BF16)
    low = (value - high.astype(F32)).astype(BF16)
    return high, low


def swap_blocks(parts):
    block = lax.broadcasted_iota(jnp.int32, parts[0].shape, 1) // (LANES // 4)

    def exchange(parts, bit):
        upper = (block & bit) != 0
        shift = bit * (LANES // 4)
        new = list(parts)
        for low in range(4):
            if low & bit:
                continue
            high = low | bit
            new[low] = jnp.where(upper, pltpu.roll(parts[high], shift, 1), parts[low])
            new[high] = jnp.where(upper, parts[high], pltpu.roll(parts[low], LANES - shift, 1))
        return new

    return exchange(exchange(parts, 2), 1)


def gather_kernel(query, key, value, cotangent, taps, out):
    groups, rows, positions = out.shape
    lanes = rows // 3
    tap_rows, channels = taps.shape
    step = pl.program_id(0)

    def place(start, array):
        turned = array.T.astype(BF16)
        out[:, start : start + lanes, :] = turned.reshape(groups, lanes, positions)

    place(0, key[...].astype(F32) * value[...].astype(F32))
    place(lanes, cotangent[...].astype(F32) * query[...].astype(F32))
    for half in range(2):
        pieces = [
            taps[:, pl.ds(pl.multiple_of(tp * (channels // 8) + step * LANES, LANES), LANES)]
            for tp in range(4 * half, 4 * half + 4)
        ]
        turned = jnp.concatenate(pieces, 0).astype(F32).T.reshape(groups, 4, 8, LANES)
        swapped = swap_blocks([turned[:, one].reshape(groups * 8, LANES) for one in range(4)])
        column = slice(half * LANES, (half + 1) * LANES)
        whole = jnp.stack([part.reshape(groups, 8, LANES) for part in swapped], 1)
        out[:, 2 * lanes :, column] = whole.reshape(groups, lanes, LANES).astype(BF16)


def scatter_kernel(
    query, key, value, cotangent, back, block_output, grad_query, grad_key, grad_value, grad_filter
):
    groups, rows, positions = back.shape
    lanes = rows // 3
    tap_rows, channels = grad_filter.shape
    step = pl.program_id(0)

    def take(start):
        wide = back[:, start : start + lanes, :].astype(F32)
        return wide.reshape(groups * lanes, positions).T

    convolved = take(0)
    block_output[...] = (query[...].astype(F32) * convolved).astype(BF16)
    grad_query[...] = (cotangent[...].astype(F32) * convolved).astype(BF16)
    adjoint = take(lanes)
    grad_key[...] = (adjoint * value[...].astype(F32)).astype(BF16)
    grad_value[...] = (adjoint * key[...].astype(F32)).astype(BF16)
    for half in range(2):
        column = slice(half * LANES, (half + 1) * LANES)
        wide = back[:, 2 * lanes :, column].astype(F32).reshape(groups, 4, 8, LANES)
        swapped = swap_blocks([wide[:, one].reshape(groups * 8, LANES) for one in range(4)])
        whole = jnp.stack([part.reshape(groups, 8, LANES) for part in swapped], 1)
        turned = whole.reshape(groups * lanes, LANES).T.astype(BF16)
        for one in range(4):
            start = (4 * half + one) * (channels // 8) + step * LANES
            grad_filter[:, pl.ds(pl.multiple_of(start, LANES), LANES)] = turned[
                one * tap_rows : (one + 1) * tap_rows
            ]


def forward(channel, lanes, first, twist_real, twist_imag, ahead, stage, spec):
    @pl.loop(0, lanes // 2, unroll=True)
    def _(pair):
        even_one, odd_one = channel(2 * pair)
        even_two, odd_two = channel(2 * pair + 1)
        both = jnp.concatenate(
            [
                jnp.concatenate([even_one, even_two], 1),
                jnp.concatenate([odd_one, odd_two], 1),
            ],
            0,
        ).astype(BF16)
        turned = jnp.dot(
            first[...], jnp.concatenate([both, both], 0), preferred_element_type=F32
        )
        real, imag = turned[:KEPT], turned[KEPT:]
        new_real = real * twist_real[...] - imag * twist_imag[...]
        new_imag = imag * twist_real[...] + real * twist_imag[...]
        at = pl.multiple_of(pair * 2 * KEPT, 2 * KEPT)
        stage[pl.ds(at, KEPT), :LANES] = new_real[:, :LANES]
        stage[pl.ds(at, KEPT), LANES:] = new_imag[:, :LANES]
        stage[pl.ds(at + KEPT, KEPT), :LANES] = new_real[:, LANES:]
        stage[pl.ds(at + KEPT, KEPT), LANES:] = new_imag[:, LANES:]

    @pl.loop(0, lanes // CHUNK, unroll=True)
    def _(step):
        at = pl.ds(pl.multiple_of(step * CHUNK * KEPT, CHUNK * KEPT), CHUNK * KEPT)
        high, low = split_value(stage[at, :])
        spec[at, :] = jnp.dot(
            jnp.concatenate([high, low, high], 1), ahead[...], preferred_element_type=F32
        )


def backward(left, right, sign, put, lanes, twist_real, twist_imag, back, last, stage):
    @pl.loop(0, lanes // CHUNK, unroll=True)
    def _(step):
        at = pl.ds(pl.multiple_of(step * CHUNK * KEPT, CHUNK * KEPT), CHUNK * KEPT)
        left_real, left_imag = left[at, :LANES], left[at, LANES:]
        right_real, right_imag = right[at, :LANES], sign * right[at, LANES:]
        real = left_real * right_real - left_imag * right_imag
        imag = left_real * right_imag + left_imag * right_real
        high, low = split_value(jnp.concatenate([real, imag], 1))
        turned = jnp.dot(
            jnp.concatenate([high, low, high], 1), back[...], preferred_element_type=F32
        )
        for one in range(CHUNK):
            real = turned[one * KEPT : (one + 1) * KEPT, :LANES]
            imag = turned[one * KEPT : (one + 1) * KEPT, LANES:]
            cos, sin = twist_real[:, :LANES], twist_imag[:, :LANES]
            row = pl.ds(pl.multiple_of((step * CHUNK + one) * KEPT, KEPT), KEPT)
            stage[row, :LANES] = real * cos + imag * sin
            stage[row, LANES:] = imag * cos - real * sin

    @pl.loop(0, lanes // 2, unroll=True)
    def _(pair):
        at = pl.multiple_of(pair * 2 * KEPT, 2 * KEPT)
        one = stage[pl.ds(at, KEPT), :]
        two = stage[pl.ds(at + KEPT, KEPT), :]
        both = jnp.concatenate(
            [
                jnp.concatenate([one[:, :LANES], two[:, :LANES]], 1),
                jnp.concatenate([one[:, LANES:], two[:, LANES:]], 1),
            ],
            0,
        )
        high, low = split_value(both)
        signal = jnp.dot(
            last[...], jnp.concatenate([high, low, high], 0), preferred_element_type=F32
        )
        blocks = signal.shape[0] // 2
        for which in range(2):
            half = signal[:, which * LANES : (which + 1) * LANES]
            put(2 * pair + which, half[:blocks], half[blocks:])


def first_kernel(
    received, first, twist_real, twist_imag, ahead, back, last, grad_filter, spec_x, spec_g, even, odd, stage
):
    sources, rows, positions = received.shape
    lanes = rows // 2

    def spectrum(start, spec):
        whole = received[:, start : start + lanes, :].astype(F32).reshape(sources * lanes, positions)
        even[...] = whole[:, :LANES]
        odd[...] = whole[:, LANES:]

        def channel(index):
            row = pl.ds(index, sources, stride=lanes)
            return even[row, :], odd[row, :]

        forward(channel, lanes, first, twist_real, twist_imag, ahead, stage, spec)

    def put(index, even_part, odd_part):
        row = pl.ds(index // 8 * (sources * 8) + index % 8, sources, stride=8)
        even[row, :] = even_part
        odd[row, :] = odd_part

    spectrum(0, spec_x)
    spectrum(lanes, spec_g)
    backward(spec_g, spec_x, -1.0, put, lanes, twist_real, twist_imag, back, last, stage)
    tall = sources * 8
    for half, holder in enumerate((even, odd)):
        swapped = swap_blocks([holder[one * tall : (one + 1) * tall, :] for one in range(4)])
        for one in range(4):
            grad_filter[4 * half + one] = swapped[one].astype(BF16)


def second_kernel(
    taps, spec_x, spec_g, first, twist_real, twist_imag, ahead, back, last, out, even, odd, stage, spec_h
):
    sources, rows, positions = out.shape
    lanes = rows // 2
    tall = sources * 8
    for half, holder in enumerate((even, odd)):
        swapped = swap_blocks([taps[4 * half + one].astype(F32) for one in range(4)])
        for one in range(4):
            holder[one * tall : (one + 1) * tall, :] = swapped[one]

    def channel(index):
        row = pl.ds(index // 8 * tall + index % 8, sources, stride=8)
        return even[row, :], odd[row, :]

    def put(index, even_part, odd_part):
        row = pl.ds(index, sources, stride=lanes)
        even[row, :] = even_part
        odd[row, :] = odd_part

    def result(start, left, right, sign):
        backward(left, right, sign, put, lanes, twist_real, twist_imag, back, last, stage)
        whole = jnp.concatenate([even[...], odd[...]], 1).astype(BF16)
        out[:, start : start + lanes, :] = whole.reshape(sources, lanes, positions)

    forward(channel, lanes, first, twist_real, twist_imag, ahead, stage, spec_h)
    result(0, spec_h, spec_x, 1.0)
    result(lanes, spec_g, spec_h, -1.0)


def gather(query, key, value, cotangent, taps, ranks):
    positions, width = query.shape
    lanes = width // ranks
    groups = LANES // lanes
    column = pl.BlockSpec((positions, LANES), lambda i: (0, i))
    return pl.pallas_call(
        gather_kernel,
        grid=(width // LANES,),
        in_specs=[column] * 4 + [pl.BlockSpec(taps.shape, lambda i: (0, 0))],
        out_specs=pl.BlockSpec((groups, 3 * lanes, positions), lambda i: (i, 0, 0)),
        out_shape=jax.ShapeDtypeStruct((ranks, 3 * lanes, positions), BF16),
        compiler_params=pltpu.CompilerParams(vmem_limit_bytes=24 * MIB),
        cost_estimate=pl.CostEstimate(flops=10**6, bytes_accessed=4 * MIB, transcendentals=0),
    )(query, key, value, cotangent, taps)


def scatter(query, key, value, cotangent, back, taps_shape):
    positions, width = query.shape
    ranks, rows, _ = back.shape
    groups = LANES // (width // ranks)
    column = pl.BlockSpec((positions, LANES), lambda i: (0, i))
    return pl.pallas_call(
        scatter_kernel,
        grid=(width // LANES,),
        in_specs=[column] * 4 + [pl.BlockSpec((groups, rows, positions), lambda i: (i, 0, 0))],
        out_specs=[column] * 4 + [pl.BlockSpec(taps_shape, lambda i: (0, 0))],
        out_shape=[jax.ShapeDtypeStruct((positions, width), BF16)] * 4
        + [jax.ShapeDtypeStruct(taps_shape, BF16)],
        compiler_params=pltpu.CompilerParams(vmem_limit_bytes=24 * MIB),
        cost_estimate=pl.CostEstimate(flops=10**6, bytes_accessed=6 * MIB, transcendentals=0),
    )(query, key, value, cotangent, back)


def whole_spec(shape):
    return pl.BlockSpec(shape, lambda i: (0,) * len(shape))


def first_part(received, tables):
    sources, rows, positions = received.shape
    lanes = rows // 3
    plain = pltpu.VMEM((sources * lanes, LANES), F32)
    spectra = (lanes * KEPT, 2 * LANES)
    shapes = [(8, sources * 8, LANES), spectra, spectra]
    return pl.pallas_call(
        first_kernel,
        grid=(1,),
        in_specs=[whole_spec((sources, 2 * lanes, positions))]
        + [whole_spec(table.shape) for table in tables],
        out_specs=[whole_spec(shape) for shape in shapes],
        out_shape=[jax.ShapeDtypeStruct(shapes[0], BF16)]
        + [jax.ShapeDtypeStruct(shape, F32) for shape in shapes[1:]],
        scratch_shapes=[plain, plain, pltpu.VMEM(spectra, F32)],
        compiler_params=pltpu.CompilerParams(vmem_limit_bytes=40 * MIB),
        cost_estimate=pl.CostEstimate(flops=5 * 10**9, bytes_accessed=8 * MIB, transcendentals=0),
    )(received, *tables)


def second_part(taps, spec_x, spec_g, tables, sources, positions):
    lanes = spec_x.shape[0] // KEPT
    plain = pltpu.VMEM((sources * lanes, LANES), F32)
    operands = [taps, spec_x, spec_g, *tables]
    return pl.pallas_call(
        second_kernel,
        grid=(1,),
        in_specs=[whole_spec(operand.shape) for operand in operands],
        out_specs=whole_spec((sources, 2 * lanes, positions)),
        out_shape=jax.ShapeDtypeStruct((sources, 3 * lanes, positions), BF16),
        scratch_shapes=[plain, plain] + [pltpu.VMEM(spec_x.shape, F32)] * 2,
        compiler_params=pltpu.CompilerParams(vmem_limit_bytes=40 * MIB),
        cost_estimate=pl.CostEstimate(flops=5 * 10**9, bytes_accessed=8 * MIB, transcendentals=0),
    )(*operands)


def local(query_proj, key_proj, value_proj, cotangent, filter_taps):
    ranks = lax.axis_size("ctx")
    sent = gather(query_proj, key_proj, value_proj, cotangent, filter_taps, ranks)
    received = lax.all_to_all(sent, "ctx", split_axis=0, concat_axis=0, tiled=True)
    _, rows, positions = received.shape
    lanes = rows // 3
    tables = [jnp.asarray(table) for table in make_tables(ranks * positions)]
    taps = received[:, 2 * lanes :].reshape(ranks, 4, 8, 2, LANES).transpose(3, 1, 0, 2, 4)
    taps = lax.all_to_all(
        taps.reshape(8, ranks * 8, LANES), "tp", split_axis=0, concat_axis=0, tiled=True
    )
    grad_filter, spec_x, spec_g = first_part(received, tables)
    grad_filter = lax.all_to_all(grad_filter, "tp", split_axis=0, concat_axis=0, tiled=True)
    made = second_part(taps, spec_x, spec_g, tables, ranks, positions)
    grad_filter = grad_filter.reshape(2, 4, ranks, 8, LANES).transpose(2, 1, 3, 0, 4)
    made = made.at[:, 2 * lanes :].set(grad_filter.reshape(ranks, lanes, positions))
    back = lax.all_to_all(made, "ctx", split_axis=0, concat_axis=0, tiled=True)
    return scatter(query_proj, key_proj, value_proj, cotangent, back, filter_taps.shape)


def solution(mesh):
    placed = (P("ctx", "tp"),) * 4 + (P(("ctx", "tp"), None),)
    return jax.shard_map(local, mesh=mesh, in_specs=placed, out_specs=placed, check_vma=False)
```

```python
import functools
import math

import jax
import jax.numpy as jnp
import ml_dtypes
import numpy as np
from jax import lax
from jax.experimental import pallas as pl
from jax.experimental.pallas import tpu as pltpu
from jax.sharding import PartitionSpec as P

F32 = jnp.float32
BF16 = jnp.bfloat16
LANES = 128
KEPT = 72
MIB = 1 << 20
UNROLL = 8
UNROLL_PAIR = 16
CHUNK = 4
COLUMNS = 512


def split_table(table):
    high = table.astype(ml_dtypes.bfloat16)
    low = (table - high.astype(np.float64)).astype(ml_dtypes.bfloat16)
    return high, low


def make_tables(seq_len):
    radix = 2 * seq_len // LANES
    blocks = radix // 2
    total = 2 * seq_len
    kept = radix // 2 + 1
    order = np.concatenate([np.arange(0, blocks, 2), np.arange(1, blocks, 2)])
    k1 = np.arange(KEPT)
    live = (k1 < kept).astype(np.float64)
    turn = 2 * math.pi * np.outer(k1, order) / radix
    first = np.concatenate([np.cos(turn) * live[:, None], -np.sin(turn) * live[:, None]], 0)
    first_table = np.concatenate(split_table(first), 1)
    lane = np.arange(LANES)
    twist = 2 * math.pi * np.outer(k1, lane) / total
    twist_real = np.tile(np.cos(twist), (1, 2)).astype(np.float32)
    twist_imag = np.tile(-np.sin(twist), (1, 2)).astype(np.float32)
    inner = 2 * math.pi * np.outer(lane, lane) / LANES
    cos, sin = np.cos(inner), np.sin(inner)
    ahead = split_table(np.block([[cos, -sin], [sin, cos]]))
    ahead_table = np.concatenate([ahead[0], ahead[0], ahead[1]], 0)
    back = split_table(np.block([[cos, sin], [-sin, cos]]))
    back_table = np.concatenate([back[0], back[0], back[1]], 0)
    weight = np.where((k1 == 0) | (k1 == radix // 2), 1.0, 2.0) * live
    weight = weight * seq_len ** (-0.5) / total
    last = split_table(np.concatenate([np.cos(turn.T) * weight, -np.sin(turn.T) * weight], 1))
    last_table = np.concatenate([last[0], last[0], last[1]], 1)
    return first_table, twist_real, twist_imag, ahead_table, back_table, last_table


def split_value(value):
    high = value.astype(BF16)
    low = (value - high.astype(F32)).astype(BF16)
    return high, low


def swap_blocks(parts):
    block = lax.broadcasted_iota(jnp.int32, parts[0].shape, 1) // (LANES // 4)

    def exchange(parts, bit):
        upper = (block & bit) != 0
        shift = bit * (LANES // 4)
        new = list(parts)
        for low in range(4):
            if low & bit:
                continue
            high = low | bit
            new[low] = jnp.where(upper, pltpu.roll(parts[high], shift, 1), parts[low])
            new[high] = jnp.where(upper, parts[high], pltpu.roll(parts[low], LANES - shift, 1))
        return new

    return exchange(exchange(parts, 2), 1)


def pair_rows(left, right):
    low = lax.broadcasted_iota(jnp.int32, left.shape, 1) < 4
    return (
        jnp.where(low, left, pltpu.roll(right, 4, 1)),
        jnp.where(low, pltpu.roll(left, 4, 1), right),
    )


def gather_kernel(query, key, value, cotangent, taps, out):
    width = query.shape[1]
    channels = taps.shape[1]
    step = pl.program_id(0)

    def interleave(left, right):
        left, right = pair_rows(left.reshape(-1, 8, LANES), right.reshape(-1, 8, LANES))
        return jnp.stack([left, right], 1).reshape(-1, 8, LANES)

    def turn(array):
        turned = array.T
        return interleave(turned[:, :LANES], turned[:, LANES:])

    def turn_taps(part):
        def some(first):
            pieces = []
            for tp in range(first, 8, 2):
                start = tp * (channels // 8) + step * width + part * LANES
                pieces.append(taps[:, pl.ds(pl.multiple_of(start, LANES), LANES)])
            return jnp.concatenate(pieces, 0).astype(F32).T

        return interleave(some(0), some(1))

    for part in range(width // LANES):
        column = slice(part * LANES, (part + 1) * LANES)
        gated = key[:, column].astype(F32) * value[:, column].astype(F32)
        grad = cotangent[:, column].astype(F32) * query[:, column].astype(F32)
        whole = jnp.concatenate([turn(gated), turn(grad), turn_taps(part)], 1)
        rows = whole.shape[0] * 24
        out[part * rows : (part + 1) * rows, :] = whole.reshape(rows, LANES).astype(BF16)


def scatter_kernel(
    query, key, value, cotangent, back, block_output, grad_query, grad_key, grad_value, grad_filter
):
    width = query.shape[1]
    tap_rows, channels = grad_filter.shape
    step = pl.program_id(0)

    def separate(array):
        array = array.reshape(-1, 2, 8, LANES)
        left, right = pair_rows(array[:, 0], array[:, 1])
        return left.reshape(-1, LANES), right.reshape(-1, LANES)

    def turn(array):
        return jnp.concatenate(separate(array), 1).T

    for part in range(width // LANES):
        column = slice(part * LANES, (part + 1) * LANES)
        rows = LANES // 4 * 24
        whole = back[part * rows : (part + 1) * rows, :].astype(F32).reshape(-1, 24, LANES)
        convolved = turn(whole[:, :8])
        block_output[:, column] = (query[:, column].astype(F32) * convolved).astype(BF16)
        grad_query[:, column] = (cotangent[:, column].astype(F32) * convolved).astype(BF16)
        adjoint = turn(whole[:, 8:16])
        grad_key[:, column] = (adjoint * value[:, column].astype(F32)).astype(BF16)
        grad_value[:, column] = (adjoint * key[:, column].astype(F32)).astype(BF16)
        for first, taps in enumerate(separate(whole[:, 16:])):
            turned = taps.T.astype(BF16)
            for one in range(4):
                start = (2 * one + first) * (channels // 8) + step * width + part * LANES
                grad_filter[:, pl.ds(pl.multiple_of(start, LANES), LANES)] = turned[
                    one * tap_rows : (one + 1) * tap_rows
                ]


def long_kernel(
    received, first, twist_real, twist_imag, ahead, back, last, out,
    arrived, leaving, taps_even, taps_odd, grad_even, grad_odd,
    stage_x, stage_g, stage_h, spec_x, spec_g, spec_h,
):
    groups = 8
    sources = received.shape[0] // (groups * 24)
    tall = sources * 8
    whole = received[...].astype(F32).reshape(sources * groups, 24, LANES)
    arrived[...] = whole[:, :16].reshape(sources * groups * 16, LANES)
    taps = whole[:, 16:].reshape(sources, groups, 8, LANES)
    for half, holder in enumerate((taps_even, taps_odd)):
        swapped = swap_blocks([taps[:, 4 * half + q].reshape(tall, LANES) for q in range(4)])
        for one in range(4):
            holder[one * tall : (one + 1) * tall, :] = swapped[one]

    def lanes_of(array):
        return array[:, :LANES], array[:, LANES:]

    def beside(one, two):
        return jnp.concatenate([one, two], 1)

    def wide_dot(array, table):
        high, low = split_value(array)
        return jnp.dot(
            jnp.concatenate([high, low, high], 1), table[...], preferred_element_type=F32
        )

    def rows_of(channel, count=1):
        return pl.ds(pl.multiple_of(channel * KEPT, KEPT), count * KEPT)

    def spaced(channel, start):
        return pl.ds(channel // 4 * 16 + channel % 4 + start, sources, stride=groups * 16)

    def tapped(channel):
        return pl.ds(channel // 8 * tall + channel % 8, sources, stride=8)

    def forward(load, stage, spec):
        @pl.loop(0, groups * 2, unroll=UNROLL_PAIR)
        def _(pair):
            even_one, odd_one = load(2 * pair)
            even_two, odd_two = load(2 * pair + 1)
            both = jnp.concatenate(
                [beside(even_one, even_two), beside(odd_one, odd_two)], 0
            ).astype(BF16)
            turned = jnp.dot(
                first[...], jnp.concatenate([both, both], 0), preferred_element_type=F32
            )
            real, imag = turned[:KEPT], turned[KEPT:]
            new_real = lanes_of(real * twist_real[...] - imag * twist_imag[...])
            new_imag = lanes_of(imag * twist_real[...] + real * twist_imag[...])
            for which in range(2):
                stage[rows_of(2 * pair + which), :LANES] = new_real[which]
                stage[rows_of(2 * pair + which), LANES:] = new_imag[which]

        @pl.loop(0, groups * 4 // CHUNK, unroll=UNROLL)
        def _(step):
            at = rows_of(step * CHUNK, CHUNK)
            spec[at, :] = wide_dot(stage[at, :], ahead)

    def backward(left, right, sign, stage, store):
        @pl.loop(0, groups * 4 // CHUNK, unroll=UNROLL)
        def _(step):
            at = rows_of(step * CHUNK, CHUNK)
            left_real, left_imag = lanes_of(left[at, :])
            right_real, right_imag = lanes_of(right[at, :])
            right_imag = sign * right_imag
            turned = wide_dot(
                beside(
                    left_real * right_real - left_imag * right_imag,
                    left_real * right_imag + left_imag * right_real,
                ),
                back,
            )
            cos, sin = twist_real[:, :LANES], twist_imag[:, :LANES]
            for one in range(CHUNK):
                real, imag = lanes_of(turned[one * KEPT : (one + 1) * KEPT])
                stage[rows_of(step * CHUNK + one), :LANES] = real * cos + imag * sin
                stage[rows_of(step * CHUNK + one), LANES:] = imag * cos - real * sin

        @pl.loop(0, groups * 2, unroll=UNROLL_PAIR)
        def _(pair):
            one_real, one_imag = lanes_of(stage[rows_of(2 * pair), :])
            two_real, two_imag = lanes_of(stage[rows_of(2 * pair + 1), :])
            high, low = split_value(
                jnp.concatenate([beside(one_real, two_real), beside(one_imag, two_imag)], 0)
            )
            signal = jnp.dot(
                last[...], jnp.concatenate([high, low, high], 0), preferred_element_type=F32
            )
            for which, half in enumerate(lanes_of(signal)):
                store(2 * pair + which, half[:sources], half[sources:])

    def load_from(start):
        return lambda channel: (
            arrived[spaced(channel, start), :],
            arrived[spaced(channel, start + 4), :],
        )

    def store_at(start):
        def store(channel, even, odd):
            leaving[spaced(channel, start), :] = even
            leaving[spaced(channel, start + 4), :] = odd

        return store

    def load_taps(channel):
        return taps_even[tapped(channel), :], taps_odd[tapped(channel), :]

    def store_grad(channel, even, odd):
        grad_even[tapped(channel), :] = even
        grad_odd[tapped(channel), :] = odd

    forward(load_from(0), stage_x, spec_x)
    forward(load_from(8), stage_g, spec_g)
    forward(load_taps, stage_h, spec_h)
    backward(spec_g, spec_x, -1.0, stage_x, store_grad)
    backward(spec_h, spec_x, 1.0, stage_g, store_at(0))
    backward(spec_g, spec_h, -1.0, stage_h, store_at(8))

    pieces = []
    for holder in (grad_even, grad_odd):
        swapped = swap_blocks([holder[one * tall : (one + 1) * tall, :] for one in range(4)])
        pieces += [piece.reshape(sources, 8, LANES) for piece in swapped]
    grad = jnp.stack(pieces, 1).reshape(sources * groups, 8, LANES)
    made = jnp.concatenate([leaving[...].reshape(sources * groups, 16, LANES), grad], 1)
    out[...] = made.reshape(received.shape).astype(BF16)


def gather(query, key, value, cotangent, taps, ranks):
    positions, width = query.shape
    column = pl.BlockSpec((positions, COLUMNS), lambda i: (0, i))
    steps = width // COLUMNS
    return pl.pallas_call(
        gather_kernel,
        grid=(steps,),
        in_specs=[column] * 4 + [pl.BlockSpec(taps.shape, lambda i: (0, 0))],
        out_specs=pl.BlockSpec((ranks * 24 // steps, LANES), lambda i: (i, 0)),
        out_shape=jax.ShapeDtypeStruct((ranks * 24, LANES), BF16),
        compiler_params=pltpu.CompilerParams(vmem_limit_bytes=60 * MIB),
        cost_estimate=pl.CostEstimate(flops=10**6, bytes_accessed=4 * MIB, transcendentals=0),
    )(query, key, value, cotangent, taps)


def scatter(query, key, value, cotangent, back, taps_shape):
    positions, width = query.shape
    column = pl.BlockSpec((positions, COLUMNS), lambda i: (0, i))
    steps = width // COLUMNS
    return pl.pallas_call(
        scatter_kernel,
        grid=(steps,),
        in_specs=[column] * 4 + [pl.BlockSpec((back.shape[0] // steps, LANES), lambda i: (i, 0))],
        out_specs=[column] * 4 + [pl.BlockSpec(taps_shape, lambda i: (0, 0))],
        out_shape=[jax.ShapeDtypeStruct((positions, width), BF16)] * 4
        + [jax.ShapeDtypeStruct(taps_shape, BF16)],
        compiler_params=pltpu.CompilerParams(vmem_limit_bytes=24 * MIB),
        cost_estimate=pl.CostEstimate(flops=10**6, bytes_accessed=6 * MIB, transcendentals=0),
    )(query, key, value, cotangent, back)


def long_convolution(received, seq_len):
    tables = [jnp.asarray(table) for table in make_tables(seq_len)]
    ranks = received.shape[0] // 24
    plain = pltpu.VMEM((ranks * 16, LANES), F32)
    taps = pltpu.VMEM((ranks * 4, LANES), F32)
    spectra = pltpu.VMEM((32 * KEPT, 2 * LANES), F32)
    return pl.pallas_call(
        long_kernel,
        out_shape=jax.ShapeDtypeStruct(received.shape, BF16),
        scratch_shapes=[plain, plain, taps, taps, taps, taps] + [spectra] * 6,
        compiler_params=pltpu.CompilerParams(vmem_limit_bytes=40 * MIB),
        cost_estimate=pl.CostEstimate(flops=10**10, bytes_accessed=3 * MIB, transcendentals=0),
    )(received, *tables)


def local(query_proj, key_proj, value_proj, cotangent, filter_taps):
    everyone = ("ctx", "tp")
    ranks = lax.axis_size("ctx") * lax.axis_size("tp")
    seq_len = query_proj.shape[0] * lax.axis_size("ctx")
    sent = gather(query_proj, key_proj, value_proj, cotangent, filter_taps, ranks)
    received = lax.all_to_all(sent, everyone, split_axis=0, concat_axis=0, tiled=True)
    made = long_convolution(received, seq_len)
    back = lax.all_to_all(made, everyone, split_axis=0, concat_axis=0, tiled=True)
    return scatter(query_proj, key_proj, value_proj, cotangent, back, filter_taps.shape)


def solution(mesh):
    placed = (P("ctx", "tp"),) * 4 + (P(("ctx", "tp"), None),)
    return jax.shard_map(local, mesh=mesh, in_specs=placed, out_specs=placed, check_vma=False)
```

```python
import functools
import math

import jax
import jax.numpy as jnp
import ml_dtypes
import numpy as np
from jax import lax
from jax.experimental import pallas as pl
from jax.experimental.pallas import tpu as pltpu
from jax.sharding import PartitionSpec as P

F32 = jnp.float32
BF16 = jnp.bfloat16
LANES = 128
KEPT = 64
MIB = 1 << 20
PIECES = 2


def split_table(table):
    high = table.astype(ml_dtypes.bfloat16)
    low = (table - high.astype(np.float64)).astype(ml_dtypes.bfloat16)
    return high, low


def make_tables(seq_len):
    radix = 2 * seq_len // LANES
    blocks = radix // 2
    total = 2 * seq_len
    order = np.concatenate([np.arange(0, blocks, 2), np.arange(1, blocks, 2)])
    k1 = np.arange(KEPT)
    turn = 2 * math.pi * np.outer(k1, order) / radix
    middle = np.cos(math.pi * order)[None]
    first = np.concatenate([np.cos(turn), middle, -np.sin(turn[1:])], 0)
    first_table = np.concatenate(split_table(first), 1)
    lane = np.arange(LANES)
    twist = 2 * math.pi * np.outer(np.arange(KEPT + 1), lane) / total
    cos, sin = np.tile(np.cos(twist), (1, 2)), np.tile(-np.sin(twist), (1, 2))
    masked = np.where(k1[:, None] == 0, 0.0, cos[:KEPT])
    middle_twist = np.concatenate([cos[KEPT:], sin[KEPT:]], 0)
    twists = [table.astype(np.float32) for table in (cos[:KEPT], sin[:KEPT], masked, middle_twist)]
    inner = 2 * math.pi * np.outer(lane, lane) / LANES
    cos, sin = np.cos(inner), np.sin(inner)
    ahead = split_table(np.block([[cos, -sin], [sin, cos]]))
    ahead_table = np.concatenate([ahead[0], ahead[0], ahead[1]], 0)
    back = split_table(np.block([[cos, sin], [-sin, cos]]))
    back_table = np.concatenate([back[0], back[0], back[1]], 0)
    weight = np.where(k1 == 0, 1.0, 2.0)
    last = np.concatenate([np.cos(turn.T) * weight, middle.T, -2.0 * np.sin(turn[1:].T)], 1)
    high, low = split_table(last * (seq_len ** (-0.5) / total))
    last_table = np.block([[high, high], [low, np.zeros_like(low)]])
    return first_table, *twists, ahead_table, back_table, last_table


def split_value(value):
    high = value.astype(BF16)
    low = (value - high.astype(F32)).astype(BF16)
    return high, low


def swap_blocks(parts):
    block = lax.broadcasted_iota(jnp.int32, parts[0].shape, 1) // (LANES // 4)

    def exchange(parts, bit):
        upper = (block & bit) != 0
        shift = bit * (LANES // 4)
        new = list(parts)
        for low in range(4):
            if low & bit:
                continue
            high = low | bit
            new[low] = jnp.where(upper, pltpu.roll(parts[high], shift, 1), parts[low])
            new[high] = jnp.where(upper, parts[high], pltpu.roll(parts[low], LANES - shift, 1))
        return new

    return exchange(exchange(parts, 2), 1)


def pair_rows(left, right):
    low = lax.broadcasted_iota(jnp.int32, left.shape, 1) < 4
    return (
        jnp.where(low, left, pltpu.roll(right, 4, 1)),
        jnp.where(low, pltpu.roll(left, 4, 1), right),
    )


def gather_kernel(
    query, key, value, cotangent, taps, out, wide, taps_here, out_here, sems, taps_sem, out_sems
):
    pieces, _, _, width = wide.shape
    channels = taps.shape[1]
    rows = out.shape[0] // pieces

    def columns(piece):
        return pl.ds(piece * width, width)

    loads = [
        [
            pltpu.make_async_copy(
                array.at[:, columns(piece)], wide.at[piece, index], sems.at[piece, index]
            )
            for index, array in enumerate((key, value, cotangent, query))
        ]
        for piece in range(pieces)
    ]
    taps_load = pltpu.make_async_copy(taps, taps_here, taps_sem)
    stores = [
        pltpu.make_async_copy(
            out_here.at[pl.ds(piece * rows, rows)],
            out.at[pl.ds(piece * rows, rows)],
            out_sems.at[piece],
        )
        for piece in range(pieces)
    ]
    for piece in range(pieces):
        for load in loads[piece]:
            load.start()
        if piece == 0:
            taps_load.start()

    def interleave(left, right):
        left, right = pair_rows(left.reshape(-1, 8, LANES), right.reshape(-1, 8, LANES))
        return jnp.stack([left, right], 1).reshape(-1, 8, LANES)

    def turn(left, right):
        turned = (left.astype(F32) * right.astype(F32)).astype(BF16).T.astype(F32)
        return interleave(turned[:, :LANES], turned[:, LANES:])

    def turn_taps(start):
        def some(first):
            parts = []
            for tp in range(first, 8, 2):
                at = tp * (channels // 8) + start
                parts.append(taps_here[:, at : at + LANES])
            return jnp.concatenate(parts, 0).T.astype(F32)

        return interleave(some(0), some(1))

    for piece in range(pieces):
        for load in loads[piece]:
            load.wait()
        if piece == 0:
            taps_load.wait()
        for part in range(width // LANES):
            column = slice(part * LANES, (part + 1) * LANES)
            whole = jnp.concatenate(
                [
                    turn(wide[piece, 0, :, column], wide[piece, 1, :, column]),
                    turn(wide[piece, 2, :, column], wide[piece, 3, :, column]),
                    turn_taps(piece * width + part * LANES),
                ],
                1,
            )
            count = whole.shape[0] * 24
            at = piece * rows + part * count
            out_here[at : at + count, :] = whole.reshape(count, LANES).astype(BF16)
        stores[piece].start()
    for store in stores:
        store.wait()


def scatter_kernel(
    query, key, value, cotangent, back,
    block_output, grad_query, grad_key, grad_value, grad_filter,
    wide, taps_here, sems, taps_sem,
):
    pieces, _, _, width = wide.shape
    tap_rows, channels = grad_filter.shape
    rows = LANES // 4 * 24
    stores = [
        [
            pltpu.make_async_copy(
                wide.at[piece, index],
                array.at[:, pl.ds(piece * width, width)],
                sems.at[piece, index],
            )
            for index, array in enumerate((block_output, grad_query, grad_key, grad_value))
        ]
        for piece in range(pieces)
    ]
    taps_store = pltpu.make_async_copy(taps_here, grad_filter, taps_sem)

    def separate(array):
        array = array.reshape(-1, 2, 8, LANES)
        left, right = pair_rows(array[:, 0], array[:, 1])
        return left.reshape(-1, LANES), right.reshape(-1, LANES)

    def turn(array):
        return jnp.concatenate(separate(array), 1).astype(BF16).T.astype(F32)

    def arrived(block):
        return back[block * rows : (block + 1) * rows, :].astype(F32).reshape(-1, 24, LANES)

    for block in range(pieces * width // LANES):
        for first, taps in enumerate(separate(arrived(block)[:, 16:])):
            turned = taps.astype(BF16).T
            for one in range(4):
                at = (2 * one + first) * (channels // 8) + block * LANES
                taps_here[:, at : at + LANES] = turned[one * tap_rows : (one + 1) * tap_rows]
    taps_store.start()
    for piece in range(pieces):
        for start, factors in ((0, (query, cotangent)), (8, (value, key))):
            for part in range(width // LANES):
                block = piece * (width // LANES) + part
                column = slice(block * LANES, (block + 1) * LANES)
                signal = turn(arrived(block)[:, start : start + 8])
                for index, factor in enumerate(factors):
                    product = (factor[:, column].astype(F32) * signal).astype(BF16)
                    wide[piece, start // 4 + index, :, part * LANES : (part + 1) * LANES] = product
            for index in range(2):
                stores[piece][start // 4 + index].start()
    for piece in range(pieces):
        for store in stores[piece]:
            store.wait()
    taps_store.wait()


def long_kernel(
    received, first, twist_real, twist_imag, twist_masked, middle_twist, ahead, back, last, out,
    arrived_x, arrived_g, leaving_y, leaving_z, taps_even, taps_odd, grad_even, grad_odd, split, middles, spectra, weights,
):
    groups = 8
    channels = 32
    wide = 4
    main = channels * KEPT
    sources = received.shape[0] // (groups * 24)
    tall = sources * 8
    whole = received[...].astype(F32).reshape(sources * groups, 24, LANES)
    arrived_x[...] = whole[:, :8].reshape(sources * groups * 8, LANES)
    arrived_g[...] = whole[:, 8:16].reshape(sources * groups * 8, LANES)
    taps = whole[:, 16:].reshape(sources, groups, 8, LANES)
    for half, holder in enumerate((taps_even, taps_odd)):
        swapped = swap_blocks([taps[:, 4 * half + q].reshape(tall, LANES) for q in range(4)])
        for one in range(4):
            holder[one * tall : (one + 1) * tall, :] = swapped[one]

    def lanes_of(array):
        return array[:, :LANES], array[:, LANES:]

    def beside(one, two):
        return jnp.concatenate([one, two], 1)

    def wide_dot(high, low, table):
        return jnp.dot(
            jnp.concatenate([high, low, high], 1), table[...], preferred_element_type=F32
        )

    def spaced(channel, start):
        return pl.ds(channel // 4 * 8 + channel % 4 + start, sources, stride=groups * 8)

    def tapped(channel):
        return pl.ds(channel // 8 * tall + channel % 8, sources, stride=8)

    def load(which, channel):
        if which == 2:
            return taps_even[tapped(channel), :], taps_odd[tapped(channel), :]
        arrived = (arrived_x, arrived_g)[which]
        return arrived[spaced(channel, 0), :], arrived[spaced(channel, 4), :]

    def store(which, channel, even, odd):
        if which == 2:
            grad_even[tapped(channel), :] = even
            grad_odd[tapped(channel), :] = odd
        else:
            leaving = (leaving_y, leaving_z)[which]
            leaving[spaced(channel, 0), :] = even
            leaving[spaced(channel, 4), :] = odd

    def enter(which, pair):
        even_one, odd_one = load(which, 2 * pair)
        even_two, odd_two = load(which, 2 * pair + 1)
        both = jnp.concatenate([beside(even_one, even_two), beside(odd_one, odd_two)], 0)
        both = both.astype(BF16)
        turned = jnp.dot(
            first[...], jnp.concatenate([both, both], 0), preferred_element_type=F32
        )
        real, imag = turned[:KEPT], turned[KEPT:]
        middle = imag[:1]
        for part, array in enumerate(
            (
                real * twist_real[...] - imag * twist_imag[...],
                imag * twist_masked[...] + real * twist_imag[...],
            )
        ):
            column = slice(part * LANES, (part + 1) * LANES)
            extra = lanes_of(middle * middle_twist[part : part + 1, :])
            for level, piece in enumerate(split_value(array)):
                for one, half in enumerate(lanes_of(piece)):
                    row = (2 * pair + one) * KEPT
                    split[which, level, row : row + KEPT, column] = half
            for one in range(2):
                middles[which, 2 * pair + one : 2 * pair + one + 1, column] = extra[one]

    def transform(which, step):
        if step is None:
            high, low = split_value(middles[which])
            at = slice(main, main + channels)
        else:
            at = slice(step * wide * KEPT, (step + 1) * wide * KEPT)
            high, low = split[which, 0, at, :], split[which, 1, at, :]
        spectra[which, at, :] = wide_dot(high, low, ahead)

    factors = ((2, 0, 1.0), (1, 2, -1.0), (1, 0, -1.0))

    def product(which, step):
        left, right, sign = factors[which]
        if step is None:
            at = slice(main, main + channels)
        else:
            at = slice(step * wide * KEPT, (step + 1) * wide * KEPT)
        left_real, left_imag = lanes_of(spectra[left, at, :])
        right_real, right_imag = lanes_of(spectra[right, at, :])
        if sign > 0:
            real = left_real * right_real - left_imag * right_imag
            imag = left_imag * right_real + left_real * right_imag
        else:
            real = left_real * right_real + left_imag * right_imag
            imag = left_imag * right_real - left_real * right_imag
        turned = wide_dot(*split_value(beside(real, imag)), back)
        if step is None:
            real, imag = lanes_of(turned)
            cos, sin = middle_twist[:1, :LANES], middle_twist[1:, :LANES]
            middles[which, :, :LANES] = real * cos + imag * sin
            return
        cos, sin = twist_real[:, :LANES], twist_imag[:, :LANES]
        top = lax.broadcasted_iota(jnp.int32, (8, LANES), 0) == 0
        for one in range(wide):
            channel = step * wide + one
            real, imag = lanes_of(turned[one * KEPT : (one + 1) * KEPT])
            new_real = real * cos + imag * sin
            new_imag = imag * cos - real * sin
            middle = middles[which, channel : channel + 1, :LANES]
            new_imag = jnp.concatenate([jnp.where(top, middle, new_imag[:8]), new_imag[8:]], 0)
            column = slice(channel % 2 * LANES, (channel % 2 + 1) * LANES)
            for part, array in enumerate((new_real, new_imag)):
                for level, piece in enumerate(split_value(array)):
                    row = (channel // 2 * 4 + 2 * level + part) * KEPT
                    weights[which, row : row + KEPT, column] = piece

    def leave(which, pair):
        signal = jnp.dot(
            last[...], weights[which, pair * 4 * KEPT : (pair + 1) * 4 * KEPT, :],
            preferred_element_type=F32,
        )
        signal = signal[: 2 * sources] + signal[2 * sources :]
        for one, half in enumerate(lanes_of(signal)):
            store(which, 2 * pair + one, half[:sources], half[sources:])

    def run(*lines):
        longest = max(len(line) for line in lines)
        for index in range(longest):
            for line in lines:
                low, high = index * len(line) // longest, (index + 1) * len(line) // longest
                for task, *where in line[low:high]:
                    task(*where)

    pairs = range(channels // 2)
    steps = [None, *range(channels // wide)]

    def line(task, which):
        return [(task, which, place) for place in (pairs if task in (enter, leave) else steps)]

    run(line(enter, 0))
    run(line(transform, 0), line(enter, 1))
    run(line(transform, 1), line(enter, 2))
    run(line(transform, 2), line(product, 2))
    run(line(product, 0), line(leave, 2))
    run(line(product, 1), line(leave, 0))
    run(line(leave, 1))

    pieces = []
    for holder in (grad_even, grad_odd):
        swapped = swap_blocks([holder[one * tall : (one + 1) * tall, :] for one in range(4)])
        pieces += [piece.reshape(sources, 8, LANES) for piece in swapped]
    grad = jnp.stack(pieces, 1).reshape(sources * groups, 8, LANES)
    shape = (sources * groups, 8, LANES)
    made = jnp.concatenate([leaving_y[...].reshape(shape), leaving_z[...].reshape(shape), grad], 1)
    out[...] = made.reshape(received.shape).astype(BF16)


def gather(query, key, value, cotangent, taps, ranks):
    positions, width = query.shape
    pieces = PIECES
    anywhere = pl.BlockSpec(memory_space=pl.ANY)
    return pl.pallas_call(
        gather_kernel,
        in_specs=[anywhere] * 5,
        out_specs=anywhere,
        out_shape=jax.ShapeDtypeStruct((ranks * 24, LANES), BF16),
        scratch_shapes=[
            pltpu.VMEM((pieces, 4, positions, width // pieces), BF16),
            pltpu.VMEM(taps.shape, BF16),
            pltpu.VMEM((ranks * 24, LANES), BF16),
            pltpu.SemaphoreType.DMA((pieces, 4)),
            pltpu.SemaphoreType.DMA,
            pltpu.SemaphoreType.DMA((pieces,)),
        ],
        compiler_params=pltpu.CompilerParams(vmem_limit_bytes=60 * MIB),
        cost_estimate=pl.CostEstimate(flops=10**6, bytes_accessed=4 * MIB, transcendentals=0),
    )(query, key, value, cotangent, taps)


def scatter(query, key, value, cotangent, back, taps_shape):
    positions, width = query.shape
    pieces = PIECES
    anywhere = pl.BlockSpec(memory_space=pl.ANY)
    return pl.pallas_call(
        scatter_kernel,
        out_specs=[anywhere] * 5,
        out_shape=[jax.ShapeDtypeStruct((positions, width), BF16)] * 4
        + [jax.ShapeDtypeStruct(taps_shape, BF16)],
        scratch_shapes=[
            pltpu.VMEM((pieces, 4, positions, width // pieces), BF16),
            pltpu.VMEM(taps_shape, BF16),
            pltpu.SemaphoreType.DMA((pieces, 4)),
            pltpu.SemaphoreType.DMA,
        ],
        compiler_params=pltpu.CompilerParams(vmem_limit_bytes=24 * MIB),
        cost_estimate=pl.CostEstimate(flops=10**6, bytes_accessed=6 * MIB, transcendentals=0),
    )(query, key, value, cotangent, back)


def long_convolution(received, seq_len):
    tables = [jnp.asarray(table) for table in make_tables(seq_len)]
    ranks = received.shape[0] // 24
    plain = pltpu.VMEM((ranks * 8, LANES), F32)
    taps = pltpu.VMEM((ranks * 4, LANES), F32)
    pair_lanes = 2 * LANES
    return pl.pallas_call(
        long_kernel,
        out_shape=jax.ShapeDtypeStruct(received.shape, BF16),
        scratch_shapes=[plain] * 4 + [taps] * 4
        + [
            pltpu.VMEM((3, 2, 32 * KEPT, pair_lanes), BF16),
            pltpu.VMEM((3, 32, pair_lanes), F32),
            pltpu.VMEM((3, 32 * KEPT + 32, pair_lanes), F32),
            pltpu.VMEM((3, 64 * KEPT, pair_lanes), BF16),
        ],
        compiler_params=pltpu.CompilerParams(vmem_limit_bytes=40 * MIB),
        cost_estimate=pl.CostEstimate(flops=10**10, bytes_accessed=3 * MIB, transcendentals=0),
    )(received, *tables)


def local(query_proj, key_proj, value_proj, cotangent, filter_taps):
    everyone = ("ctx", "tp")
    ranks = lax.axis_size("ctx") * lax.axis_size("tp")
    seq_len = query_proj.shape[0] * lax.axis_size("ctx")
    sent = gather(query_proj, key_proj, value_proj, cotangent, filter_taps, ranks)
    received = lax.all_to_all(sent, everyone, split_axis=0, concat_axis=0, tiled=True)
    made = long_convolution(received, seq_len)
    back = lax.all_to_all(made, everyone, split_axis=0, concat_axis=0, tiled=True)
    return scatter(query_proj, key_proj, value_proj, cotangent, back, filter_taps.shape)


def solution(mesh):
    placed = (P("ctx", "tp"),) * 4 + (P(("ctx", "tp"), None),)
    return jax.shard_map(local, mesh=mesh, in_specs=placed, out_specs=placed, check_vma=False)
```

```python
import functools
import math

import jax
import jax.numpy as jnp
import ml_dtypes
import numpy as np
from jax import lax
from jax.experimental import pallas as pl
from jax.experimental.pallas import tpu as pltpu
from jax.sharding import PartitionSpec as P

F32 = jnp.float32
BF16 = jnp.bfloat16
LANES = 128
KEPT = 64
MIB = 1 << 20
PIECES = 2


def split_table(table):
    high = table.astype(ml_dtypes.bfloat16)
    low = (table - high.astype(np.float64)).astype(ml_dtypes.bfloat16)
    return high, low


def make_tables(seq_len):
    radix = 2 * seq_len // LANES
    blocks = radix // 2
    total = 2 * seq_len
    order = np.concatenate([np.arange(0, blocks, 2), np.arange(1, blocks, 2)])
    k1 = np.arange(KEPT)
    turn = 2 * math.pi * np.outer(k1, order) / radix
    middle = np.cos(math.pi * order)[None]
    first = np.concatenate([np.cos(turn), middle, -np.sin(turn[1:])], 0)
    first_table = np.concatenate(split_table(first), 1)
    lane = np.arange(LANES)
    twist = 2 * math.pi * np.outer(np.arange(KEPT + 1), lane) / total
    cos, sin = np.tile(np.cos(twist), (1, 2)), np.tile(-np.sin(twist), (1, 2))
    masked = np.where(k1[:, None] == 0, 0.0, cos[:KEPT])
    middle_twist = np.concatenate([cos[KEPT:], sin[KEPT:]], 0)
    twists = [table.astype(np.float32) for table in (cos[:KEPT], sin[:KEPT], masked, middle_twist)]
    inner = 2 * math.pi * np.outer(lane, lane) / LANES
    cos, sin = np.cos(inner), np.sin(inner)
    ahead = split_table(np.block([[cos, -sin], [sin, cos]]))
    ahead_table = np.concatenate([ahead[0], ahead[0], ahead[1]], 0)
    back = split_table(np.block([[cos, sin], [-sin, cos]]))
    back_table = np.concatenate([back[0], back[0], back[1]], 0)
    weight = np.where(k1 == 0, 1.0, 2.0)
    last = np.concatenate([np.cos(turn.T) * weight, middle.T, -2.0 * np.sin(turn[1:].T)], 1)
    high, low = split_table(last * (seq_len ** (-0.5) / total))
    last_table = np.block([[high, high], [low, np.zeros_like(low)]])
    return first_table, *twists, ahead_table, back_table, last_table


def split_value(value):
    high = value.astype(BF16)
    low = (value - high.astype(F32)).astype(BF16)
    return high, low


def swap_blocks(parts):
    block = lax.broadcasted_iota(jnp.int32, parts[0].shape, 1) // (LANES // 4)

    def exchange(parts, bit):
        upper = (block & bit) != 0
        shift = bit * (LANES // 4)
        new = list(parts)
        for low in range(4):
            if low & bit:
                continue
            high = low | bit
            new[low] = jnp.where(upper, pltpu.roll(parts[high], shift, 1), parts[low])
            new[high] = jnp.where(upper, parts[high], pltpu.roll(parts[low], LANES - shift, 1))
        return new

    return exchange(exchange(parts, 2), 1)


def pair_rows(left, right):
    low = lax.broadcasted_iota(jnp.int32, left.shape, 1) < 4
    return (
        jnp.where(low, left, pltpu.roll(right, 4, 1)),
        jnp.where(low, pltpu.roll(left, 4, 1), right),
    )


def gather_kernel(
    query, key, value, cotangent, taps, out, wide, taps_here, out_here, sems, taps_sem, out_sems
):
    pieces, _, _, width = wide.shape
    channels = taps.shape[1]
    rows = out.shape[0] // pieces

    def columns(piece):
        return pl.ds(piece * width, width)

    loads = [
        [
            pltpu.make_async_copy(
                array.at[:, columns(piece)], wide.at[piece, index], sems.at[piece, index]
            )
            for index, array in enumerate((key, value, cotangent, query))
        ]
        for piece in range(pieces)
    ]
    taps_load = pltpu.make_async_copy(taps, taps_here, taps_sem)
    stores = [
        pltpu.make_async_copy(
            out_here.at[pl.ds(piece * rows, rows)],
            out.at[pl.ds(piece * rows, rows)],
            out_sems.at[piece],
        )
        for piece in range(pieces)
    ]
    for piece in range(pieces):
        for load in loads[piece]:
            load.start()
        if piece == 0:
            taps_load.start()

    def interleave(left, right):
        left, right = pair_rows(left.reshape(-1, 8, LANES), right.reshape(-1, 8, LANES))
        return jnp.stack([left, right], 1).reshape(-1, 8, LANES)

    def turn(left, right):
        turned = (left.astype(F32) * right.astype(F32)).astype(BF16).T.astype(F32)
        return interleave(turned[:, :LANES], turned[:, LANES:])

    def turn_taps(start):
        def some(first):
            parts = []
            for tp in range(first, 8, 2):
                at = tp * (channels // 8) + start
                parts.append(taps_here[:, at : at + LANES])
            return jnp.concatenate(parts, 0).T.astype(F32)

        return interleave(some(0), some(1))

    for piece in range(pieces):
        for load in loads[piece]:
            load.wait()
        if piece == 0:
            taps_load.wait()
        for part in range(width // LANES):
            column = slice(part * LANES, (part + 1) * LANES)
            whole = jnp.concatenate(
                [
                    turn(wide[piece, 0, :, column], wide[piece, 1, :, column]),
                    turn(wide[piece, 2, :, column], wide[piece, 3, :, column]),
                    turn_taps(piece * width + part * LANES),
                ],
                1,
            )
            count = whole.shape[0] * 24
            at = piece * rows + part * count
            out_here[at : at + count, :] = whole.reshape(count, LANES).astype(BF16)
        stores[piece].start()
    for store in stores:
        store.wait()


def scatter_kernel(
    query, key, value, cotangent, back,
    block_output, grad_query, grad_key, grad_value, grad_filter,
    wide, taps_here, sems, taps_sem,
):
    pieces, _, _, width = wide.shape
    tap_rows, channels = grad_filter.shape
    rows = LANES // 4 * 24
    stores = [
        [
            pltpu.make_async_copy(
                wide.at[piece, index],
                array.at[:, pl.ds(piece * width, width)],
                sems.at[piece, index],
            )
            for index, array in enumerate((block_output, grad_query, grad_key, grad_value))
        ]
        for piece in range(pieces)
    ]
    taps_store = pltpu.make_async_copy(taps_here, grad_filter, taps_sem)

    def separate(array):
        array = array.reshape(-1, 2, 8, LANES)
        left, right = pair_rows(array[:, 0], array[:, 1])
        return left.reshape(-1, LANES), right.reshape(-1, LANES)

    def turn(array):
        return jnp.concatenate(separate(array), 1).astype(BF16).T.astype(F32)

    def arrived(block):
        return back[block * rows : (block + 1) * rows, :].astype(F32).reshape(-1, 24, LANES)

    for block in range(pieces * width // LANES):
        for first, taps in enumerate(separate(arrived(block)[:, 16:])):
            turned = taps.astype(BF16).T
            for one in range(4):
                at = (2 * one + first) * (channels // 8) + block * LANES
                taps_here[:, at : at + LANES] = turned[one * tap_rows : (one + 1) * tap_rows]
    taps_store.start()
    for piece in range(pieces):
        for start, factors in ((0, (query, cotangent)), (8, (value, key))):
            for part in range(width // LANES):
                block = piece * (width // LANES) + part
                column = slice(block * LANES, (block + 1) * LANES)
                signal = turn(arrived(block)[:, start : start + 8])
                for index, factor in enumerate(factors):
                    product = (factor[:, column].astype(F32) * signal).astype(BF16)
                    wide[piece, start // 4 + index, :, part * LANES : (part + 1) * LANES] = product
            for index in range(2):
                stores[piece][start // 4 + index].start()
    for piece in range(pieces):
        for store in stores[piece]:
            store.wait()
    taps_store.wait()


def long_kernel(
    received, first, twist_real, twist_imag, twist_masked, middle_twist, ahead, back, last, out,
    arrived_x, arrived_g, leaving_y, leaving_z, taps_even, taps_odd, grad_even, grad_odd, split, middles, spectra, weights,
):
    groups = 8
    channels = 32
    wide = 4
    main = channels * KEPT
    sources = received.shape[0] // (groups * 24)
    tall = sources * 8
    whole = received[...].astype(F32).reshape(sources * groups, 24, LANES)
    tight = groups * 8
    pitch = tight + 1
    whole = whole.reshape(sources, groups, 24, LANES)
    for source in range(sources):
        at = slice(source * pitch, source * pitch + tight)
        arrived_x[at, :] = whole[source, :, :8].reshape(tight, LANES)
        arrived_g[at, :] = whole[source, :, 8:16].reshape(tight, LANES)
    taps = whole[:, :, 16:]
    for half, holder in enumerate((taps_even, taps_odd)):
        swapped = swap_blocks([taps[:, 4 * half + q].reshape(tall, LANES) for q in range(4)])
        for one in range(4):
            for source in range(sources):
                at = (one * sources + source) * 9
                holder[at : at + 8, :] = swapped[one][source * 8 : (source + 1) * 8]

    def lanes_of(array):
        return array[:, :LANES], array[:, LANES:]

    def beside(one, two):
        return jnp.concatenate([one, two], 1)

    def wide_dot(high, low, table):
        return jnp.dot(
            jnp.concatenate([high, low, high], 1), table[...], preferred_element_type=F32
        )

    def spaced(channel, start):
        return pl.ds(channel // 4 * 8 + channel % 4 + start, sources, stride=pitch)

    def tapped(channel):
        return pl.ds(channel // 8 * (sources * 9) + channel % 8, sources, stride=9)

    def load(which, channel):
        if which == 2:
            return taps_even[tapped(channel), :], taps_odd[tapped(channel), :]
        arrived = (arrived_x, arrived_g)[which]
        return arrived[spaced(channel, 0), :], arrived[spaced(channel, 4), :]

    def store(which, channel, even, odd):
        if which == 2:
            grad_even[tapped(channel), :] = even
            grad_odd[tapped(channel), :] = odd
        else:
            leaving = (leaving_y, leaving_z)[which]
            leaving[spaced(channel, 0), :] = even
            leaving[spaced(channel, 4), :] = odd

    def enter(which, pair):
        even_one, odd_one = load(which, 2 * pair)
        even_two, odd_two = load(which, 2 * pair + 1)
        both = jnp.concatenate([beside(even_one, even_two), beside(odd_one, odd_two)], 0)
        both = both.astype(BF16)
        turned = jnp.dot(
            first[...], jnp.concatenate([both, both], 0), preferred_element_type=F32
        )
        real, imag = turned[:KEPT], turned[KEPT:]
        middle = imag[:1]
        for part, array in enumerate(
            (
                real * twist_real[...] - imag * twist_imag[...],
                imag * twist_masked[...] + real * twist_imag[...],
            )
        ):
            column = slice(part * LANES, (part + 1) * LANES)
            extra = lanes_of(middle * middle_twist[part : part + 1, :])
            for level, piece in enumerate(split_value(array)):
                for one, half in enumerate(lanes_of(piece)):
                    row = (2 * pair + one) * KEPT
                    split[which, level, row : row + KEPT, column] = half
            for one in range(2):
                middles[which, 2 * pair + one : 2 * pair + one + 1, column] = extra[one]

    def transform(which, step):
        if step is None:
            high, low = split_value(middles[which])
            at = slice(main, main + channels)
        else:
            at = slice(step * wide * KEPT, (step + 1) * wide * KEPT)
            high, low = split[which, 0, at, :], split[which, 1, at, :]
        spectra[which, at, :] = wide_dot(high, low, ahead)

    factors = ((2, 0, 1.0), (1, 2, -1.0), (1, 0, -1.0))

    def product(which, step):
        left, right, sign = factors[which]
        if step is None:
            at = slice(main, main + channels)
        else:
            at = slice(step * wide * KEPT, (step + 1) * wide * KEPT)
        left_real, left_imag = lanes_of(spectra[left, at, :])
        right_real, right_imag = lanes_of(spectra[right, at, :])
        if sign > 0:
            real = left_real * right_real - left_imag * right_imag
            imag = left_imag * right_real + left_real * right_imag
        else:
            real = left_real * right_real + left_imag * right_imag
            imag = left_imag * right_real - left_real * right_imag
        turned = wide_dot(*split_value(beside(real, imag)), back)
        if step is None:
            real, imag = lanes_of(turned)
            cos, sin = middle_twist[:1, :LANES], middle_twist[1:, :LANES]
            middles[which, :, :LANES] = real * cos + imag * sin
            return
        cos, sin = twist_real[:, :LANES], twist_imag[:, :LANES]
        top = lax.broadcasted_iota(jnp.int32, (8, LANES), 0) == 0
        for one in range(wide):
            channel = step * wide + one
            real, imag = lanes_of(turned[one * KEPT : (one + 1) * KEPT])
            new_real = real * cos + imag * sin
            new_imag = imag * cos - real * sin
            middle = middles[which, channel : channel + 1, :LANES]
            new_imag = jnp.concatenate([jnp.where(top, middle, new_imag[:8]), new_imag[8:]], 0)
            column = slice(channel % 2 * LANES, (channel % 2 + 1) * LANES)
            for part, array in enumerate((new_real, new_imag)):
                for level, piece in enumerate(split_value(array)):
                    row = (channel // 2 * 4 + 2 * level + part) * KEPT
                    weights[which, row : row + KEPT, column] = piece

    def leave(which, pair):
        signal = jnp.dot(
            last[...], weights[which, pair * 4 * KEPT : (pair + 1) * 4 * KEPT, :],
            preferred_element_type=F32,
        )
        signal = signal[: 2 * sources] + signal[2 * sources :]
        for one, half in enumerate(lanes_of(signal)):
            store(which, 2 * pair + one, half[:sources], half[sources:])

    def run(*lines):
        longest = max(len(line) for line in lines)
        for index in range(longest):
            for line in lines:
                low, high = index * len(line) // longest, (index + 1) * len(line) // longest
                for task, *where in line[low:high]:
                    task(*where)

    pairs = range(channels // 2)
    steps = [None, *range(channels // wide)]

    def line(task, which):
        return [(task, which, place) for place in (pairs if task in (enter, leave) else steps)]

    run(line(enter, 0))
    run(line(transform, 0), line(enter, 1))
    run(line(transform, 1), line(enter, 2))
    run(line(transform, 2), line(product, 2))
    run(line(product, 0), line(leave, 2))
    run(line(product, 1), line(leave, 0))
    run(line(leave, 1))

    def loose(holder, first, count, size):
        starts = [(first + index) * (size + 1) for index in range(count)]
        return [holder[start : start + size, :] for start in starts]

    pieces = []
    for holder in (grad_even, grad_odd):
        swapped = swap_blocks(
            [jnp.concatenate(loose(holder, one * sources, sources, 8), 0) for one in range(4)]
        )
        pieces += [piece.reshape(sources, 8, LANES) for piece in swapped]
    grad = jnp.stack(pieces, 1).reshape(sources * groups, 8, LANES)
    made = [
        jnp.concatenate(loose(holder, 0, sources, tight), 0).reshape(sources * groups, 8, LANES)
        for holder in (leaving_y, leaving_z)
    ]
    out[...] = jnp.concatenate([*made, grad], 1).reshape(received.shape).astype(BF16)


def gather(query, key, value, cotangent, taps, ranks):
    positions, width = query.shape
    pieces = PIECES
    anywhere = pl.BlockSpec(memory_space=pl.ANY)
    return pl.pallas_call(
        gather_kernel,
        in_specs=[anywhere] * 5,
        out_specs=anywhere,
        out_shape=jax.ShapeDtypeStruct((ranks * 24, LANES), BF16),
        scratch_shapes=[
            pltpu.VMEM((pieces, 4, positions, width // pieces), BF16),
            pltpu.VMEM(taps.shape, BF16),
            pltpu.VMEM((ranks * 24, LANES), BF16),
            pltpu.SemaphoreType.DMA((pieces, 4)),
            pltpu.SemaphoreType.DMA,
            pltpu.SemaphoreType.DMA((pieces,)),
        ],
        compiler_params=pltpu.CompilerParams(vmem_limit_bytes=60 * MIB),
        cost_estimate=pl.CostEstimate(flops=10**6, bytes_accessed=4 * MIB, transcendentals=0),
    )(query, key, value, cotangent, taps)


def scatter(query, key, value, cotangent, back, taps_shape):
    positions, width = query.shape
    pieces = PIECES
    anywhere = pl.BlockSpec(memory_space=pl.ANY)
    return pl.pallas_call(
        scatter_kernel,
        out_specs=[anywhere] * 5,
        out_shape=[jax.ShapeDtypeStruct((positions, width), BF16)] * 4
        + [jax.ShapeDtypeStruct(taps_shape, BF16)],
        scratch_shapes=[
            pltpu.VMEM((pieces, 4, positions, width // pieces), BF16),
            pltpu.VMEM(taps_shape, BF16),
            pltpu.SemaphoreType.DMA((pieces, 4)),
            pltpu.SemaphoreType.DMA,
        ],
        compiler_params=pltpu.CompilerParams(vmem_limit_bytes=24 * MIB),
        cost_estimate=pl.CostEstimate(flops=10**6, bytes_accessed=6 * MIB, transcendentals=0),
    )(query, key, value, cotangent, back)


def long_convolution(received, seq_len):
    tables = [jnp.asarray(table) for table in make_tables(seq_len)]
    ranks = received.shape[0] // 24
    plain = pltpu.VMEM((ranks // 8 * 65 + 7, LANES), F32)
    taps = pltpu.VMEM((ranks // 2 * 9, LANES), F32)
    pair_lanes = 2 * LANES
    return pl.pallas_call(
        long_kernel,
        out_shape=jax.ShapeDtypeStruct(received.shape, BF16),
        scratch_shapes=[plain] * 4 + [taps] * 4
        + [
            pltpu.VMEM((3, 2, 32 * KEPT, pair_lanes), BF16),
            pltpu.VMEM((3, 32, pair_lanes), F32),
            pltpu.VMEM((3, 32 * KEPT + 32, pair_lanes), F32),
            pltpu.VMEM((3, 64 * KEPT, pair_lanes), BF16),
        ],
        compiler_params=pltpu.CompilerParams(vmem_limit_bytes=40 * MIB),
        cost_estimate=pl.CostEstimate(flops=10**10, bytes_accessed=3 * MIB, transcendentals=0),
    )(received, *tables)


def local(query_proj, key_proj, value_proj, cotangent, filter_taps):
    everyone = ("ctx", "tp")
    ranks = lax.axis_size("ctx") * lax.axis_size("tp")
    seq_len = query_proj.shape[0] * lax.axis_size("ctx")
    sent = gather(query_proj, key_proj, value_proj, cotangent, filter_taps, ranks)
    received = lax.all_to_all(sent, everyone, split_axis=0, concat_axis=0, tiled=True)
    made = long_convolution(received, seq_len)
    back = lax.all_to_all(made, everyone, split_axis=0, concat_axis=0, tiled=True)
    return scatter(query_proj, key_proj, value_proj, cotangent, back, filter_taps.shape)


def solution(mesh):
    placed = (P("ctx", "tp"),) * 4 + (P(("ctx", "tp"), None),)
    return jax.shard_map(local, mesh=mesh, in_specs=placed, out_specs=placed, check_vma=False)
```

```python
import functools
import math

import jax
import jax.numpy as jnp
import ml_dtypes
import numpy as np
from jax import lax
from jax.experimental import pallas as pl
from jax.experimental.pallas import tpu as pltpu
from jax.sharding import PartitionSpec as P

F32 = jnp.float32
BF16 = jnp.bfloat16
LANES = 128
KEPT = 64
MIB = 1 << 20
PIECES = 2


def split_table(table):
    high = table.astype(ml_dtypes.bfloat16)
    low = (table - high.astype(np.float64)).astype(ml_dtypes.bfloat16)
    return high, low


def make_tables(seq_len):
    radix = 2 * seq_len // LANES
    blocks = radix // 2
    total = 2 * seq_len
    order = np.concatenate([np.arange(0, blocks, 2), np.arange(1, blocks, 2)])
    k1 = np.arange(KEPT)
    turn = 2 * math.pi * np.outer(k1, order) / radix
    middle = np.cos(math.pi * order)[None]
    first = np.concatenate([np.cos(turn), middle, -np.sin(turn[1:])], 0)
    first_table = np.concatenate(split_table(first), 1)
    lane = np.arange(LANES)
    twist = 2 * math.pi * np.outer(np.arange(KEPT + 1), lane) / total
    cos, sin = np.cos(twist), -np.sin(twist)
    masked = np.where(k1[:, None] == 0, 0.0, cos[:KEPT])
    middle_twist = np.concatenate([cos[KEPT:], sin[KEPT:]], 0)
    twists = [table.astype(np.float32) for table in (cos[:KEPT], sin[:KEPT], masked, middle_twist)]
    inner = 2 * math.pi * np.outer(lane, lane) / LANES
    cos, sin = np.cos(inner), np.sin(inner)
    ahead = split_table(np.block([[cos, -sin], [sin, cos]]))
    ahead_table = np.concatenate([ahead[0], ahead[0], ahead[1]], 0)
    back = split_table(np.block([[cos, sin], [-sin, cos]]))
    back_table = np.concatenate([back[0], back[0], back[1]], 0)
    weight = np.where(k1 == 0, 1.0, 2.0)
    last = np.concatenate([np.cos(turn.T) * weight, middle.T, -2.0 * np.sin(turn[1:].T)], 1)
    high, low = split_table(last * (seq_len ** (-0.5) / total))
    last_table = np.block([[high, high], [low, np.zeros_like(low)]])
    return first_table, *twists, ahead_table, back_table, last_table


def split_value(value):
    high = value.astype(BF16)
    low = (value - high.astype(F32)).astype(BF16)
    return high, low


def swap_blocks(parts):
    block = lax.broadcasted_iota(jnp.int32, parts[0].shape, 1) // (LANES // 4)

    def exchange(parts, bit):
        upper = (block & bit) != 0
        shift = bit * (LANES // 4)
        new = list(parts)
        for low in range(4):
            if low & bit:
                continue
            high = low | bit
            new[low] = jnp.where(upper, pltpu.roll(parts[high], shift, 1), parts[low])
            new[high] = jnp.where(upper, parts[high], pltpu.roll(parts[low], LANES - shift, 1))
        return new

    return exchange(exchange(parts, 2), 1)


def pair_rows(left, right):
    low = lax.broadcasted_iota(jnp.int32, left.shape, 1) < 4
    return (
        jnp.where(low, left, pltpu.roll(right, 4, 1)),
        jnp.where(low, pltpu.roll(left, 4, 1), right),
    )


def gather_kernel(
    query, key, value, cotangent, taps, out, wide, taps_here, out_here, sems, taps_sem, out_sems
):
    pieces, _, _, width = wide.shape
    channels = taps.shape[1]
    rows = out.shape[0] // pieces

    def columns(piece):
        return pl.ds(piece * width, width)

    loads = [
        [
            pltpu.make_async_copy(
                array.at[:, columns(piece)], wide.at[piece, index], sems.at[piece, index]
            )
            for index, array in enumerate((key, value, cotangent, query))
        ]
        for piece in range(pieces)
    ]
    taps_load = pltpu.make_async_copy(taps, taps_here, taps_sem)
    stores = [
        pltpu.make_async_copy(
            out_here.at[pl.ds(piece * rows, rows)],
            out.at[pl.ds(piece * rows, rows)],
            out_sems.at[piece],
        )
        for piece in range(pieces)
    ]
    for piece in range(pieces):
        for load in loads[piece]:
            load.start()
        if piece == 0:
            taps_load.start()

    def interleave(left, right):
        left, right = pair_rows(left.reshape(-1, 8, LANES), right.reshape(-1, 8, LANES))
        return jnp.stack([left, right], 1).reshape(-1, 8, LANES)

    def turn(left, right):
        turned = (left.astype(F32) * right.astype(F32)).astype(BF16).T.astype(F32)
        return interleave(turned[:, :LANES], turned[:, LANES:])

    def turn_taps(start):
        def some(first):
            parts = []
            for tp in range(first, 8, 2):
                at = tp * (channels // 8) + start
                parts.append(taps_here[:, at : at + LANES])
            return jnp.concatenate(parts, 0).T.astype(F32)

        return interleave(some(0), some(1))

    for piece in range(pieces):
        for load in loads[piece]:
            load.wait()
        if piece == 0:
            taps_load.wait()
        for part in range(width // LANES):
            column = slice(part * LANES, (part + 1) * LANES)
            whole = jnp.concatenate(
                [
                    turn(wide[piece, 0, :, column], wide[piece, 1, :, column]),
                    turn(wide[piece, 2, :, column], wide[piece, 3, :, column]),
                    turn_taps(piece * width + part * LANES),
                ],
                1,
            )
            count = whole.shape[0] * 24
            at = piece * rows + part * count
            out_here[at : at + count, :] = whole.reshape(count, LANES).astype(BF16)
        stores[piece].start()
    for store in stores:
        store.wait()


def scatter_kernel(
    query, key, value, cotangent, back,
    block_output, grad_query, grad_key, grad_value, grad_filter,
    wide, taps_here, sems, taps_sem,
):
    pieces, _, _, width = wide.shape
    tap_rows, channels = grad_filter.shape
    rows = LANES // 4 * 24
    stores = [
        [
            pltpu.make_async_copy(
                wide.at[piece, index],
                array.at[:, pl.ds(piece * width, width)],
                sems.at[piece, index],
            )
            for index, array in enumerate((block_output, grad_query, grad_key, grad_value))
        ]
        for piece in range(pieces)
    ]
    taps_store = pltpu.make_async_copy(taps_here, grad_filter, taps_sem)

    def separate(array):
        array = array.reshape(-1, 2, 8, LANES)
        left, right = pair_rows(array[:, 0], array[:, 1])
        return left.reshape(-1, LANES), right.reshape(-1, LANES)

    def turn(array):
        return jnp.concatenate(separate(array), 1).astype(BF16).T.astype(F32)

    def arrived(block):
        return back[block * rows : (block + 1) * rows, :].astype(F32).reshape(-1, 24, LANES)

    for block in range(pieces * width // LANES):
        for first, taps in enumerate(separate(arrived(block)[:, 16:])):
            turned = taps.astype(BF16).T
            for one in range(4):
                at = (2 * one + first) * (channels // 8) + block * LANES
                taps_here[:, at : at + LANES] = turned[one * tap_rows : (one + 1) * tap_rows]
    taps_store.start()
    for piece in range(pieces):
        for start, factors in ((0, (query, cotangent)), (8, (value, key))):
            for part in range(width // LANES):
                block = piece * (width // LANES) + part
                column = slice(block * LANES, (block + 1) * LANES)
                signal = turn(arrived(block)[:, start : start + 8])
                for index, factor in enumerate(factors):
                    product = (factor[:, column].astype(F32) * signal).astype(BF16)
                    wide[piece, start // 4 + index, :, part * LANES : (part + 1) * LANES] = product
            for index in range(2):
                stores[piece][start // 4 + index].start()
    for piece in range(pieces):
        for store in stores[piece]:
            store.wait()
    taps_store.wait()


def long_kernel(
    received, first, twist_real, twist_imag, twist_masked, middle_twist, ahead, back, last, out,
    arrived_x, arrived_g, leaving_y, leaving_z, taps_even, taps_odd, grad_even, grad_odd, split, middles, spectra, weights,
):
    groups = 8
    channels = 32
    wide = 4
    main = channels * KEPT
    sources = received.shape[0] // (groups * 24)
    tall = sources * 8
    whole = received[...].astype(F32).reshape(sources * groups, 24, LANES)
    tight = groups * 8
    pitch = tight + 1
    whole = whole.reshape(sources, groups, 24, LANES)
    for source in range(sources):
        at = slice(source * pitch, source * pitch + tight)
        arrived_x[at, :] = whole[source, :, :8].reshape(tight, LANES)
        arrived_g[at, :] = whole[source, :, 8:16].reshape(tight, LANES)
    taps = whole[:, :, 16:]
    for half, holder in enumerate((taps_even, taps_odd)):
        swapped = swap_blocks([taps[:, 4 * half + q].reshape(tall, LANES) for q in range(4)])
        for one in range(4):
            for source in range(sources):
                at = (one * sources + source) * 9
                holder[at : at + 8, :] = swapped[one][source * 8 : (source + 1) * 8]

    def lanes_of(array):
        return array[:, :LANES], array[:, LANES:]

    def beside(one, two):
        return jnp.concatenate([one, two], 1)

    def wide_dot(high, low, table):
        return jnp.dot(
            jnp.concatenate([high, low, high], 1), table[...], preferred_element_type=F32
        )

    def spaced(channel, start):
        return pl.ds(channel // 4 * 8 + channel % 4 + start, sources, stride=pitch)

    def tapped(channel):
        return pl.ds(channel // 8 * (sources * 9) + channel % 8, sources, stride=9)

    def load(which, channel):
        if which == 2:
            return taps_even[tapped(channel), :], taps_odd[tapped(channel), :]
        arrived = (arrived_x, arrived_g)[which]
        return arrived[spaced(channel, 0), :], arrived[spaced(channel, 4), :]

    def store(which, channel, even, odd):
        if which == 2:
            grad_even[tapped(channel), :] = even
            grad_odd[tapped(channel), :] = odd
        else:
            leaving = (leaving_y, leaving_z)[which]
            leaving[spaced(channel, 0), :] = even
            leaving[spaced(channel, 4), :] = odd

    def enter(which, pair):
        even_one, odd_one = load(which, 2 * pair)
        even_two, odd_two = load(which, 2 * pair + 1)
        both = jnp.concatenate([beside(even_one, even_two), beside(odd_one, odd_two)], 0)
        both = both.astype(BF16)
        turned = jnp.dot(
            first[...], jnp.concatenate([both, both], 0), preferred_element_type=F32
        )
        cos, sin, masked = twist_real[...], twist_imag[...], twist_masked[...]
        for one, half in enumerate(lanes_of(turned)):
            real, imag = half[:KEPT], half[KEPT:]
            row = (2 * pair + one) * KEPT
            parts = (real * cos - imag * sin, imag * masked + real * sin)
            for part, array in enumerate(parts):
                column = slice(part * LANES, (part + 1) * LANES)
                for level, piece in enumerate(split_value(array)):
                    split[which, level, row : row + KEPT, column] = piece
                middles[which, 2 * pair + one : 2 * pair + one + 1, column] = (
                    imag[:1] * middle_twist[part : part + 1, :]
                )

    def transform(which, step):
        if step is None:
            high, low = split_value(middles[which])
            at = slice(main, main + channels)
        else:
            at = slice(step * wide * KEPT, (step + 1) * wide * KEPT)
            high, low = split[which, 0, at, :], split[which, 1, at, :]
        spectra[which, at, :] = wide_dot(high, low, ahead)

    factors = ((2, 0, 1.0), (1, 2, -1.0), (1, 0, -1.0))

    def product(which, step):
        left, right, sign = factors[which]
        if step is None:
            at = slice(main, main + channels)
        else:
            at = slice(step * wide * KEPT, (step + 1) * wide * KEPT)
        left_real, left_imag = lanes_of(spectra[left, at, :])
        right_real, right_imag = lanes_of(spectra[right, at, :])
        if sign > 0:
            real = left_real * right_real - left_imag * right_imag
            imag = left_imag * right_real + left_real * right_imag
        else:
            real = left_real * right_real + left_imag * right_imag
            imag = left_imag * right_real - left_real * right_imag
        turned = wide_dot(*split_value(beside(real, imag)), back)
        if step is None:
            real, imag = lanes_of(turned)
            cos, sin = middle_twist[:1, :], middle_twist[1:, :]
            middles[which, :, :LANES] = real * cos + imag * sin
            return
        cos, sin = twist_real[...], twist_imag[...]
        top = lax.broadcasted_iota(jnp.int32, (8, LANES), 0) == 0
        for one in range(wide):
            channel = step * wide + one
            real, imag = lanes_of(turned[one * KEPT : (one + 1) * KEPT])
            new_real = real * cos + imag * sin
            new_imag = imag * cos - real * sin
            middle = middles[which, channel : channel + 1, :LANES]
            new_imag = jnp.concatenate([jnp.where(top, middle, new_imag[:8]), new_imag[8:]], 0)
            column = slice(channel % 2 * LANES, (channel % 2 + 1) * LANES)
            for part, array in enumerate((new_real, new_imag)):
                for level, piece in enumerate(split_value(array)):
                    row = (channel // 2 * 4 + 2 * level + part) * KEPT
                    weights[which, row : row + KEPT, column] = piece

    def leave(which, pair):
        signal = jnp.dot(
            last[...], weights[which, pair * 4 * KEPT : (pair + 1) * 4 * KEPT, :],
            preferred_element_type=F32,
        )
        signal = signal[: 2 * sources] + signal[2 * sources :]
        for one, half in enumerate(lanes_of(signal)):
            store(which, 2 * pair + one, half[:sources], half[sources:])

    def run(*lines):
        longest = max(len(line) for line in lines)
        for index in range(longest):
            for line in lines:
                low, high = index * len(line) // longest, (index + 1) * len(line) // longest
                for task, *where in line[low:high]:
                    task(*where)

    pairs = range(channels // 2)
    steps = [None, *range(channels // wide)]

    def line(task, which):
        return [(task, which, place) for place in (pairs if task in (enter, leave) else steps)]

    run(line(enter, 0))
    run(line(enter, 1), line(transform, 0))
    run(line(enter, 2), line(transform, 1))
    run(line(transform, 2), line(product, 2))
    run(line(leave, 2), line(product, 0))
    run(line(leave, 0), line(product, 1))
    run(line(leave, 1))

    def loose(holder, first, count, size):
        starts = [(first + index) * (size + 1) for index in range(count)]
        return [holder[start : start + size, :] for start in starts]

    pieces = []
    for holder in (grad_even, grad_odd):
        swapped = swap_blocks(
            [jnp.concatenate(loose(holder, one * sources, sources, 8), 0) for one in range(4)]
        )
        pieces += [piece.reshape(sources, 8, LANES) for piece in swapped]
    grad = jnp.stack(pieces, 1).reshape(sources * groups, 8, LANES)
    made = [
        jnp.concatenate(loose(holder, 0, sources, tight), 0).reshape(sources * groups, 8, LANES)
        for holder in (leaving_y, leaving_z)
    ]
    out[...] = jnp.concatenate([*made, grad], 1).reshape(received.shape).astype(BF16)


def gather(query, key, value, cotangent, taps, ranks):
    positions, width = query.shape
    pieces = PIECES
    anywhere = pl.BlockSpec(memory_space=pl.ANY)
    return pl.pallas_call(
        gather_kernel,
        in_specs=[anywhere] * 5,
        out_specs=anywhere,
        out_shape=jax.ShapeDtypeStruct((ranks * 24, LANES), BF16),
        scratch_shapes=[
            pltpu.VMEM((pieces, 4, positions, width // pieces), BF16),
            pltpu.VMEM(taps.shape, BF16),
            pltpu.VMEM((ranks * 24, LANES), BF16),
            pltpu.SemaphoreType.DMA((pieces, 4)),
            pltpu.SemaphoreType.DMA,
            pltpu.SemaphoreType.DMA((pieces,)),
        ],
        compiler_params=pltpu.CompilerParams(vmem_limit_bytes=60 * MIB),
        cost_estimate=pl.CostEstimate(flops=10**6, bytes_accessed=4 * MIB, transcendentals=0),
    )(query, key, value, cotangent, taps)


def scatter(query, key, value, cotangent, back, taps_shape):
    positions, width = query.shape
    pieces = PIECES
    anywhere = pl.BlockSpec(memory_space=pl.ANY)
    return pl.pallas_call(
        scatter_kernel,
        out_specs=[anywhere] * 5,
        out_shape=[jax.ShapeDtypeStruct((positions, width), BF16)] * 4
        + [jax.ShapeDtypeStruct(taps_shape, BF16)],
        scratch_shapes=[
            pltpu.VMEM((pieces, 4, positions, width // pieces), BF16),
            pltpu.VMEM(taps_shape, BF16),
            pltpu.SemaphoreType.DMA((pieces, 4)),
            pltpu.SemaphoreType.DMA,
        ],
        compiler_params=pltpu.CompilerParams(vmem_limit_bytes=24 * MIB),
        cost_estimate=pl.CostEstimate(flops=10**6, bytes_accessed=6 * MIB, transcendentals=0),
    )(query, key, value, cotangent, back)


def long_convolution(received, seq_len):
    tables = [jnp.asarray(table) for table in make_tables(seq_len)]
    ranks = received.shape[0] // 24
    plain = pltpu.VMEM((ranks // 8 * 65 + 72, LANES), F32)
    taps = pltpu.VMEM((ranks // 2 * 9 + 16, LANES), F32)
    pair_lanes = 2 * LANES
    return pl.pallas_call(
        long_kernel,
        out_shape=jax.ShapeDtypeStruct(received.shape, BF16),
        scratch_shapes=[plain] * 4 + [taps] * 4
        + [
            pltpu.VMEM((3, 2, 32 * KEPT, pair_lanes), BF16),
            pltpu.VMEM((3, 32, pair_lanes), F32),
            pltpu.VMEM((3, 32 * KEPT + 32, pair_lanes), F32),
            pltpu.VMEM((3, 64 * KEPT, pair_lanes), BF16),
        ],
        compiler_params=pltpu.CompilerParams(vmem_limit_bytes=40 * MIB),
        cost_estimate=pl.CostEstimate(flops=10**10, bytes_accessed=3 * MIB, transcendentals=0),
    )(received, *tables)


def local(query_proj, key_proj, value_proj, cotangent, filter_taps):
    everyone = ("ctx", "tp")
    ranks = lax.axis_size("ctx") * lax.axis_size("tp")
    seq_len = query_proj.shape[0] * lax.axis_size("ctx")
    sent = gather(query_proj, key_proj, value_proj, cotangent, filter_taps, ranks)
    received = lax.all_to_all(sent, everyone, split_axis=0, concat_axis=0, tiled=True)
    made = long_convolution(received, seq_len)
    back = lax.all_to_all(made, everyone, split_axis=0, concat_axis=0, tiled=True)
    return scatter(query_proj, key_proj, value_proj, cotangent, back, filter_taps.shape)


def solution(mesh):
    placed = (P("ctx", "tp"),) * 4 + (P(("ctx", "tp"), None),)
    return jax.shard_map(local, mesh=mesh, in_specs=placed, out_specs=placed, check_vma=False)
```

```python
import functools
import math

import jax
import jax.numpy as jnp
import ml_dtypes
import numpy as np
from jax import lax
from jax.experimental import pallas as pl
from jax.experimental.pallas import tpu as pltpu
from jax.sharding import PartitionSpec as P

F32 = jnp.float32
BF16 = jnp.bfloat16
LANES = 128
KEPT = 64
MIB = 1 << 20
PIECES = 2


def split_table(table):
    high = table.astype(ml_dtypes.bfloat16)
    low = (table - high.astype(np.float64)).astype(ml_dtypes.bfloat16)
    return high, low


def make_tables(seq_len):
    radix = 2 * seq_len // LANES
    blocks = radix // 2
    total = 2 * seq_len
    order = np.concatenate([np.arange(0, blocks, 2), np.arange(1, blocks, 2)])
    k1 = np.arange(KEPT)
    turn = 2 * math.pi * np.outer(k1, order) / radix
    middle = np.cos(math.pi * order)[None]
    first = np.concatenate([np.cos(turn), middle, -np.sin(turn[1:])], 0)
    first_table = np.concatenate(split_table(first), 1)
    lane = np.arange(LANES)
    twist = 2 * math.pi * np.outer(np.arange(KEPT + 1), lane) / total
    cos, sin = np.cos(twist), -np.sin(twist)
    masked = np.where(k1[:, None] == 0, 0.0, cos[:KEPT])
    middle_twist = np.concatenate([cos[KEPT:], sin[KEPT:]], 0)
    twists = [table.astype(np.float32) for table in (cos[:KEPT], sin[:KEPT], masked, middle_twist)]
    inner = 2 * math.pi * np.outer(lane, lane) / LANES
    cos, sin = np.cos(inner), np.sin(inner)
    ahead = split_table(np.block([[cos, -sin], [sin, cos]]))
    ahead_table = np.concatenate([ahead[0], ahead[0], ahead[1]], 0)
    back = split_table(np.block([[cos, sin], [-sin, cos]]))
    back_table = np.concatenate([back[0], back[0], back[1]], 0)
    weight = np.where(k1 == 0, 1.0, 2.0)
    last = np.concatenate([np.cos(turn.T) * weight, middle.T, -2.0 * np.sin(turn[1:].T)], 1)
    high, low = split_table(last * (seq_len ** (-0.5) / total))
    last_table = np.block([[high, high], [low, np.zeros_like(low)]])
    return first_table, *twists, ahead_table, back_table, last_table


def split_value(value):
    high = value.astype(BF16)
    low = (value - high.astype(F32)).astype(BF16)
    return high, low


def swap_blocks(parts):
    block = lax.broadcasted_iota(jnp.int32, parts[0].shape, 1) // (LANES // 4)

    def exchange(parts, bit):
        upper = (block & bit) != 0
        shift = bit * (LANES // 4)
        new = list(parts)
        for low in range(4):
            if low & bit:
                continue
            high = low | bit
            new[low] = jnp.where(upper, pltpu.roll(parts[high], shift, 1), parts[low])
            new[high] = jnp.where(upper, parts[high], pltpu.roll(parts[low], LANES - shift, 1))
        return new

    return exchange(exchange(parts, 2), 1)


def pair_rows(left, right):
    low = lax.broadcasted_iota(jnp.int32, left.shape, 1) < 4
    return (
        jnp.where(low, left, pltpu.roll(right, 4, 1)),
        jnp.where(low, pltpu.roll(left, 4, 1), right),
    )


def gather_kernel(
    query, key, value, cotangent, taps, out, wide, taps_here, out_here, sems, taps_sem, out_sems
):
    pieces, _, _, width = wide.shape
    channels = taps.shape[1]
    parts = width // LANES
    rows = out.shape[0] // pieces // parts

    def columns(piece):
        return pl.ds(piece * width, width)

    loads = [
        [
            pltpu.make_async_copy(
                array.at[:, columns(piece)], wide.at[piece, index], sems.at[piece, index]
            )
            for index, array in enumerate((key, value, cotangent, query))
        ]
        for piece in range(pieces)
    ]
    taps_load = pltpu.make_async_copy(taps, taps_here, taps_sem)
    stores = [
        pltpu.make_async_copy(
            out_here.at[pl.ds(block * rows, rows)],
            out.at[pl.ds(block * rows, rows)],
            out_sems.at[block],
        )
        for block in range(pieces * parts)
    ]
    for piece in range(pieces):
        for load in loads[piece]:
            load.start()
        if piece == 0:
            taps_load.start()

    def interleave(left, right):
        left, right = pair_rows(left.reshape(-1, 8, LANES), right.reshape(-1, 8, LANES))
        return jnp.stack([left, right], 1).reshape(-1, 8, LANES)

    def turn(left, right):
        turned = (left.astype(F32) * right.astype(F32)).astype(BF16).T.astype(F32)
        return interleave(turned[:, :LANES], turned[:, LANES:])

    def turn_taps(start):
        def some(first):
            parts = []
            for tp in range(first, 8, 2):
                at = tp * (channels // 8) + start
                parts.append(taps_here[:, at : at + LANES])
            return jnp.concatenate(parts, 0).T.astype(F32)

        return interleave(some(0), some(1))

    for piece in range(pieces):
        for load in loads[piece]:
            load.wait()
        if piece == 0:
            taps_load.wait()
        for part in range(parts):
            column = slice(part * LANES, (part + 1) * LANES)
            whole = jnp.concatenate(
                [
                    turn(wide[piece, 0, :, column], wide[piece, 1, :, column]),
                    turn(wide[piece, 2, :, column], wide[piece, 3, :, column]),
                    turn_taps(piece * width + part * LANES),
                ],
                1,
            )
            block = piece * parts + part
            out_here[block * rows : (block + 1) * rows, :] = whole.reshape(rows, LANES).astype(BF16)
            stores[block].start()
    for store in stores:
        store.wait()


def scatter_kernel(
    query, key, value, cotangent, back,
    block_output, grad_query, grad_key, grad_value, grad_filter,
    wide, taps_here, sems, taps_sem,
):
    pieces, _, _, width = wide.shape
    tap_rows, channels = grad_filter.shape
    rows = LANES // 4 * 24
    stores = [
        [
            pltpu.make_async_copy(
                wide.at[piece, index],
                array.at[:, pl.ds(piece * width, width)],
                sems.at[piece, index],
            )
            for index, array in enumerate((block_output, grad_query, grad_key, grad_value))
        ]
        for piece in range(pieces)
    ]
    taps_store = pltpu.make_async_copy(taps_here, grad_filter, taps_sem)

    def separate(array):
        array = array.reshape(-1, 2, 8, LANES)
        left, right = pair_rows(array[:, 0], array[:, 1])
        return left.reshape(-1, LANES), right.reshape(-1, LANES)

    def turn(array):
        return jnp.concatenate(separate(array), 1).astype(BF16).T.astype(F32)

    def arrived(block):
        return back[block * rows : (block + 1) * rows, :].astype(F32).reshape(-1, 24, LANES)

    for block in range(pieces * width // LANES):
        for first, taps in enumerate(separate(arrived(block)[:, 16:])):
            turned = taps.astype(BF16).T
            for one in range(4):
                at = (2 * one + first) * (channels // 8) + block * LANES
                taps_here[:, at : at + LANES] = turned[one * tap_rows : (one + 1) * tap_rows]
    taps_store.start()
    for piece in range(pieces):
        for start, factors in ((0, (query, cotangent)), (8, (value, key))):
            for part in range(width // LANES):
                block = piece * (width // LANES) + part
                column = slice(block * LANES, (block + 1) * LANES)
                signal = turn(arrived(block)[:, start : start + 8])
                for index, factor in enumerate(factors):
                    product = (factor[:, column].astype(F32) * signal).astype(BF16)
                    wide[piece, start // 4 + index, :, part * LANES : (part + 1) * LANES] = product
            for index in range(2):
                stores[piece][start // 4 + index].start()
    for piece in range(pieces):
        for store in stores[piece]:
            store.wait()
    taps_store.wait()


def long_kernel(
    received, first, twist_real, twist_imag, twist_masked, middle_twist, ahead, back, last, out,
    arrived_x, arrived_g, leaving_y, leaving_z, taps_even, taps_odd, grad_even, grad_odd, split, middles, spectra, weights,
):
    groups = 8
    channels = 32
    wide = 8
    main = channels * KEPT
    sources = received.shape[0] // (groups * 24)
    tall = sources * 8
    whole = received[...].astype(F32).reshape(sources * groups, 24, LANES)
    tight = groups * 8
    pitch = tight + 1
    whole = whole.reshape(sources, groups, 24, LANES)
    for source in range(sources):
        at = slice(source * pitch, source * pitch + tight)
        arrived_x[at, :] = whole[source, :, :8].reshape(tight, LANES)
        arrived_g[at, :] = whole[source, :, 8:16].reshape(tight, LANES)
    taps = whole[:, :, 16:]
    for half, holder in enumerate((taps_even, taps_odd)):
        swapped = swap_blocks([taps[:, 4 * half + q].reshape(tall, LANES) for q in range(4)])
        for one in range(4):
            for source in range(sources):
                at = (one * sources + source) * 9
                holder[at : at + 8, :] = swapped[one][source * 8 : (source + 1) * 8]

    def lanes_of(array):
        return array[:, :LANES], array[:, LANES:]

    def beside(one, two):
        return jnp.concatenate([one, two], 1)

    def wide_dot(high, low, table):
        return jnp.dot(
            jnp.concatenate([high, low, high], 1), table[...], preferred_element_type=F32
        )

    def spaced(channel, start):
        return pl.ds(channel // 4 * 8 + channel % 4 + start, sources, stride=pitch)

    def tapped(channel):
        return pl.ds(channel // 8 * (sources * 9) + channel % 8, sources, stride=9)

    def load(which, channel):
        if which == 2:
            return taps_even[tapped(channel), :], taps_odd[tapped(channel), :]
        arrived = (arrived_x, arrived_g)[which]
        return arrived[spaced(channel, 0), :], arrived[spaced(channel, 4), :]

    def store(which, channel, even, odd):
        if which == 2:
            grad_even[tapped(channel), :] = even
            grad_odd[tapped(channel), :] = odd
        else:
            leaving = (leaving_y, leaving_z)[which]
            leaving[spaced(channel, 0), :] = even
            leaving[spaced(channel, 4), :] = odd

    def enter(which, pair):
        even_one, odd_one = load(which, 2 * pair)
        even_two, odd_two = load(which, 2 * pair + 1)
        both = jnp.concatenate([beside(even_one, even_two), beside(odd_one, odd_two)], 0)
        both = both.astype(BF16)
        turned = jnp.dot(
            first[...], jnp.concatenate([both, both], 0), preferred_element_type=F32
        )
        cos, sin, masked = twist_real[...], twist_imag[...], twist_masked[...]
        for one, half in enumerate(lanes_of(turned)):
            real, imag = half[:KEPT], half[KEPT:]
            row = (2 * pair + one) * KEPT
            parts = (real * cos - imag * sin, imag * masked + real * sin)
            for part, array in enumerate(parts):
                column = slice(part * LANES, (part + 1) * LANES)
                for level, piece in enumerate(split_value(array)):
                    split[which, level, row : row + KEPT, column] = piece
                middles[which, 2 * pair + one : 2 * pair + one + 1, column] = (
                    imag[:1] * middle_twist[part : part + 1, :]
                )

    def rows_of(step):
        return slice(step * wide * KEPT, (step + 1) * wide * KEPT)

    middle_rows = slice(main, main + channels)

    def transform(which, step):
        at = rows_of(step)
        high, low = split[which, 0, at, :], split[which, 1, at, :]
        if step == 0:
            extra = split_value(middles[which])
            high = jnp.concatenate([high, extra[0]], 0)
            low = jnp.concatenate([low, extra[1]], 0)
        result = wide_dot(high, low, ahead)
        spectra[which, at, :] = result[: wide * KEPT]
        if step == 0:
            spectra[which, middle_rows, :] = result[wide * KEPT :]

    factors = ((2, 0, 1.0), (1, 2, -1.0), (1, 0, -1.0))

    def product(which, step):
        left, right, sign = factors[which]

        def part_of(index):
            whole = spectra[index, rows_of(step), :]
            if step == 0:
                whole = jnp.concatenate([whole, spectra[index, middle_rows, :]], 0)
            return lanes_of(whole)

        left_real, left_imag = part_of(left)
        right_real, right_imag = part_of(right)
        if sign > 0:
            real = left_real * right_real - left_imag * right_imag
            imag = left_imag * right_real + left_real * right_imag
        else:
            real = left_real * right_real + left_imag * right_imag
            imag = left_imag * right_real - left_real * right_imag
        turned = wide_dot(*split_value(beside(real, imag)), back)
        if step == 0:
            real, imag = lanes_of(turned[wide * KEPT :])
            cos, sin = middle_twist[:1, :], middle_twist[1:, :]
            middles[3 + which, :, :LANES] = real * cos + imag * sin
        cos, sin = twist_real[...], twist_imag[...]
        top = lax.broadcasted_iota(jnp.int32, (8, LANES), 0) == 0
        for one in range(wide):
            channel = step * wide + one
            real, imag = lanes_of(turned[one * KEPT : (one + 1) * KEPT])
            new_real = real * cos + imag * sin
            new_imag = imag * cos - real * sin
            middle = middles[3 + which, channel : channel + 1, :LANES]
            new_imag = jnp.concatenate([jnp.where(top, middle, new_imag[:8]), new_imag[8:]], 0)
            column = slice(channel % 2 * LANES, (channel % 2 + 1) * LANES)
            for part, array in enumerate((new_real, new_imag)):
                for level, piece in enumerate(split_value(array)):
                    row = (channel // 2 * 4 + 2 * level + part) * KEPT
                    weights[which, row : row + KEPT, column] = piece

    def leave(which, pair):
        signal = jnp.dot(
            last[...], weights[which, pair * 4 * KEPT : (pair + 1) * 4 * KEPT, :],
            preferred_element_type=F32,
        )
        signal = signal[: 2 * sources] + signal[2 * sources :]
        for one, half in enumerate(lanes_of(signal)):
            store(which, 2 * pair + one, half[:sources], half[sources:])

    def run(*lines):
        longest = max(len(line) for line in lines)
        for index in range(longest):
            for line in lines:
                low, high = index * len(line) // longest, (index + 1) * len(line) // longest
                for task, *where in line[low:high]:
                    task(*where)

    pairs = range(channels // 2)
    steps = range(channels // wide)

    def line(task, which):
        return [(task, which, place) for place in (pairs if task in (enter, leave) else steps)]

    run(line(enter, 0))
    run(line(enter, 1), line(transform, 0))
    run(line(enter, 2), line(transform, 1))
    run(line(transform, 2), line(product, 2))
    run(line(leave, 2), line(product, 0))
    run(line(leave, 0), line(product, 1))
    run(line(leave, 1))

    def loose(holder, first, count, size):
        starts = [(first + index) * (size + 1) for index in range(count)]
        return [holder[start : start + size, :] for start in starts]

    pieces = []
    for holder in (grad_even, grad_odd):
        swapped = swap_blocks(
            [jnp.concatenate(loose(holder, one * sources, sources, 8), 0) for one in range(4)]
        )
        pieces += [piece.reshape(sources, 8, LANES) for piece in swapped]
    grad = jnp.stack(pieces, 1).reshape(sources * groups, 8, LANES)
    made = [
        jnp.concatenate(loose(holder, 0, sources, tight), 0).reshape(sources * groups, 8, LANES)
        for holder in (leaving_y, leaving_z)
    ]
    out[...] = jnp.concatenate([*made, grad], 1).reshape(received.shape).astype(BF16)


def gather(query, key, value, cotangent, taps, ranks):
    positions, width = query.shape
    pieces = PIECES
    anywhere = pl.BlockSpec(memory_space=pl.ANY)
    return pl.pallas_call(
        gather_kernel,
        in_specs=[anywhere] * 5,
        out_specs=anywhere,
        out_shape=jax.ShapeDtypeStruct((ranks * 24, LANES), BF16),
        scratch_shapes=[
            pltpu.VMEM((pieces, 4, positions, width // pieces), BF16),
            pltpu.VMEM(taps.shape, BF16),
            pltpu.VMEM((ranks * 24, LANES), BF16),
            pltpu.SemaphoreType.DMA((pieces, 4)),
            pltpu.SemaphoreType.DMA,
            pltpu.SemaphoreType.DMA((width // LANES,)),
        ],
        compiler_params=pltpu.CompilerParams(vmem_limit_bytes=60 * MIB),
        cost_estimate=pl.CostEstimate(flops=10**6, bytes_accessed=4 * MIB, transcendentals=0),
    )(query, key, value, cotangent, taps)


def scatter(query, key, value, cotangent, back, taps_shape):
    positions, width = query.shape
    pieces = PIECES
    anywhere = pl.BlockSpec(memory_space=pl.ANY)
    return pl.pallas_call(
        scatter_kernel,
        out_specs=[anywhere] * 5,
        out_shape=[jax.ShapeDtypeStruct((positions, width), BF16)] * 4
        + [jax.ShapeDtypeStruct(taps_shape, BF16)],
        scratch_shapes=[
            pltpu.VMEM((pieces, 4, positions, width // pieces), BF16),
            pltpu.VMEM(taps_shape, BF16),
            pltpu.SemaphoreType.DMA((pieces, 4)),
            pltpu.SemaphoreType.DMA,
        ],
        compiler_params=pltpu.CompilerParams(vmem_limit_bytes=24 * MIB),
        cost_estimate=pl.CostEstimate(flops=10**6, bytes_accessed=6 * MIB, transcendentals=0),
    )(query, key, value, cotangent, back)


def long_convolution(received, seq_len):
    tables = [jnp.asarray(table) for table in make_tables(seq_len)]
    ranks = received.shape[0] // 24
    plain = pltpu.VMEM((ranks // 8 * 65 + 72, LANES), F32)
    taps = pltpu.VMEM((ranks // 2 * 9 + 16, LANES), F32)
    pair_lanes = 2 * LANES
    return pl.pallas_call(
        long_kernel,
        out_shape=jax.ShapeDtypeStruct(received.shape, BF16),
        scratch_shapes=[plain] * 4 + [taps] * 4
        + [
            pltpu.VMEM((3, 2, 32 * KEPT, pair_lanes), BF16),
            pltpu.VMEM((6, 32, pair_lanes), F32),
            pltpu.VMEM((3, 32 * KEPT + 32, pair_lanes), F32),
            pltpu.VMEM((3, 64 * KEPT, pair_lanes), BF16),
        ],
        compiler_params=pltpu.CompilerParams(vmem_limit_bytes=40 * MIB),
        cost_estimate=pl.CostEstimate(flops=10**10, bytes_accessed=3 * MIB, transcendentals=0),
    )(received, *tables)


def local(query_proj, key_proj, value_proj, cotangent, filter_taps):
    everyone = ("ctx", "tp")
    ranks = lax.axis_size("ctx") * lax.axis_size("tp")
    seq_len = query_proj.shape[0] * lax.axis_size("ctx")
    sent = gather(query_proj, key_proj, value_proj, cotangent, filter_taps, ranks)
    received = lax.all_to_all(sent, everyone, split_axis=0, concat_axis=0, tiled=True)
    made = long_convolution(received, seq_len)
    back = lax.all_to_all(made, everyone, split_axis=0, concat_axis=0, tiled=True)
    return scatter(query_proj, key_proj, value_proj, cotangent, back, filter_taps.shape)


def solution(mesh):
    placed = (P("ctx", "tp"),) * 4 + (P(("ctx", "tp"), None),)
    return jax.shard_map(local, mesh=mesh, in_specs=placed, out_specs=placed, check_vma=False)
```

```python
import functools
import math

import jax
import jax.numpy as jnp
import ml_dtypes
import numpy as np
from jax import lax
from jax.experimental import pallas as pl
from jax.experimental.pallas import tpu as pltpu
from jax.sharding import PartitionSpec as P

F32 = jnp.float32
BF16 = jnp.bfloat16
LANES = 128
KEPT = 64
MIB = 1 << 20
PIECES = 2


def split_table(table):
    high = table.astype(ml_dtypes.bfloat16)
    low = (table - high.astype(np.float64)).astype(ml_dtypes.bfloat16)
    return high, low


def make_tables(seq_len):
    radix = 2 * seq_len // LANES
    blocks = radix // 2
    total = 2 * seq_len
    order = np.concatenate([np.arange(0, blocks, 2), np.arange(1, blocks, 2)])
    k1 = np.arange(KEPT)
    turn = 2 * math.pi * np.outer(k1, order) / radix
    middle = np.cos(math.pi * order)[None]
    first = np.concatenate([np.cos(turn), middle, -np.sin(turn[1:])], 0)
    first_table = np.concatenate(split_table(first), 1)
    lane = np.arange(LANES)
    twist = 2 * math.pi * np.outer(np.arange(KEPT + 1), lane) / total
    cos, sin = np.cos(twist), -np.sin(twist)
    masked = np.where(k1[:, None] == 0, 0.0, cos[:KEPT])
    middle_twist = np.concatenate([cos[KEPT:], sin[KEPT:]], 0)
    twists = [table.astype(np.float32) for table in (cos[:KEPT], sin[:KEPT], masked, middle_twist)]
    inner = 2 * math.pi * np.outer(lane, lane) / LANES
    cos, sin = np.cos(inner), np.sin(inner)
    ahead = split_table(np.block([[cos, -sin], [sin, cos]]))
    ahead_table = np.concatenate([ahead[0], ahead[0], ahead[1]], 0)
    back = split_table(np.block([[cos, sin], [-sin, cos]]))
    back_table = np.concatenate([back[0], back[0], back[1]], 0)
    weight = np.where(k1 == 0, 1.0, 2.0)
    last = np.concatenate([np.cos(turn.T) * weight, middle.T, -2.0 * np.sin(turn[1:].T)], 1)
    high, low = split_table(last * (seq_len ** (-0.5) / total))
    last_table = np.block([[high, high], [low, np.zeros_like(low)]])
    return first_table, *twists, ahead_table, back_table, last_table


def split_value(value):
    high = value.astype(BF16)
    low = (value - high.astype(F32)).astype(BF16)
    return high, low


def swap_blocks(parts):
    block = lax.broadcasted_iota(jnp.int32, parts[0].shape, 1) // (LANES // 4)

    def exchange(parts, bit):
        upper = (block & bit) != 0
        shift = bit * (LANES // 4)
        new = list(parts)
        for low in range(4):
            if low & bit:
                continue
            high = low | bit
            new[low] = jnp.where(upper, pltpu.roll(parts[high], shift, 1), parts[low])
            new[high] = jnp.where(upper, parts[high], pltpu.roll(parts[low], LANES - shift, 1))
        return new

    return exchange(exchange(parts, 2), 1)


def pair_rows(left, right):
    low = lax.broadcasted_iota(jnp.int32, left.shape, 1) < 4
    return (
        jnp.where(low, left, pltpu.roll(right, 4, 1)),
        jnp.where(low, pltpu.roll(left, 4, 1), right),
    )


def gather_kernel(
    query, key, value, cotangent, taps, out, wide, taps_here, out_here, sems, taps_sem, out_sems
):
    pieces, _, _, width = wide.shape
    channels = taps.shape[1]
    parts = width // LANES
    rows = out.shape[0] // pieces // parts

    def columns(piece):
        return pl.ds(piece * width, width)

    loads = [
        [
            pltpu.make_async_copy(
                array.at[:, columns(piece)], wide.at[piece, index], sems.at[piece, index]
            )
            for index, array in enumerate((key, value, cotangent, query))
        ]
        for piece in range(pieces)
    ]
    taps_load = pltpu.make_async_copy(taps, taps_here, taps_sem)
    stores = [
        pltpu.make_async_copy(
            out_here.at[pl.ds(block * rows, rows)],
            out.at[pl.ds(block * rows, rows)],
            out_sems.at[block],
        )
        for block in range(pieces * parts)
    ]
    for piece in range(pieces):
        for load in loads[piece]:
            load.start()
        if piece == 0:
            taps_load.start()

    def interleave(left, right):
        left, right = pair_rows(left.reshape(-1, 8, LANES), right.reshape(-1, 8, LANES))
        return jnp.stack([left, right], 1).reshape(-1, 8, LANES)

    def turn(left, right):
        turned = (left.astype(F32) * right.astype(F32)).astype(BF16).T.astype(F32)
        return interleave(turned[:, :LANES], turned[:, LANES:])

    def turn_taps(start):
        def some(first):
            parts = []
            for tp in range(first, 8, 2):
                at = tp * (channels // 8) + start
                parts.append(taps_here[:, at : at + LANES])
            return jnp.concatenate(parts, 0).T.astype(F32)

        return interleave(some(0), some(1))

    for piece in range(pieces):
        for load in loads[piece]:
            load.wait()
        if piece == 0:
            taps_load.wait()
        for part in range(parts):
            column = slice(part * LANES, (part + 1) * LANES)
            whole = jnp.concatenate(
                [
                    turn(wide[piece, 0, :, column], wide[piece, 1, :, column]),
                    turn(wide[piece, 2, :, column], wide[piece, 3, :, column]),
                    turn_taps(piece * width + part * LANES),
                ],
                1,
            )
            block = piece * parts + part
            out_here[block * rows : (block + 1) * rows, :] = whole.reshape(rows, LANES).astype(BF16)
            stores[block].start()
    for store in stores:
        store.wait()


def scatter_kernel(
    query, key, value, cotangent, back,
    block_output, grad_query, grad_key, grad_value, grad_filter,
    wide, taps_here, sems, taps_sem,
):
    pieces, _, _, width = wide.shape
    tap_rows, channels = grad_filter.shape
    rows = LANES // 4 * 24
    stores = [
        [
            pltpu.make_async_copy(
                wide.at[piece, index],
                array.at[:, pl.ds(piece * width, width)],
                sems.at[piece, index],
            )
            for index, array in enumerate((block_output, grad_query, grad_key, grad_value))
        ]
        for piece in range(pieces)
    ]
    taps_store = pltpu.make_async_copy(taps_here, grad_filter, taps_sem)

    def separate(array):
        array = array.reshape(-1, 2, 8, LANES)
        left, right = pair_rows(array[:, 0], array[:, 1])
        return left.reshape(-1, LANES), right.reshape(-1, LANES)

    def turn(array):
        return jnp.concatenate(separate(array), 1).astype(BF16).T.astype(F32)

    def arrived(block):
        return back[block * rows : (block + 1) * rows, :].astype(F32).reshape(-1, 24, LANES)

    for block in range(pieces * width // LANES):
        for first, taps in enumerate(separate(arrived(block)[:, 16:])):
            turned = taps.astype(BF16).T
            for one in range(4):
                at = (2 * one + first) * (channels // 8) + block * LANES
                taps_here[:, at : at + LANES] = turned[one * tap_rows : (one + 1) * tap_rows]
    taps_store.start()
    for piece in range(pieces):
        for start, factors in ((0, (query, cotangent)), (8, (value, key))):
            for part in range(width // LANES):
                block = piece * (width // LANES) + part
                column = slice(block * LANES, (block + 1) * LANES)
                signal = turn(arrived(block)[:, start : start + 8])
                for index, factor in enumerate(factors):
                    product = (factor[:, column].astype(F32) * signal).astype(BF16)
                    wide[piece, start // 4 + index, :, part * LANES : (part + 1) * LANES] = product
            for index in range(2):
                stores[piece][start // 4 + index].start()
    for piece in range(pieces):
        for store in stores[piece]:
            store.wait()
    taps_store.wait()


def long_kernel(
    received, first, twist_real, twist_imag, twist_masked, middle_twist, ahead, back, last, out,
    arrived_x, arrived_g, leaving_y, leaving_z, taps_even, taps_odd, grad_even, grad_odd, split, middles, spectra, weights,
):
    groups = 8
    channels = 32
    wide = 8
    main = channels * KEPT
    sources = received.shape[0] // (groups * 24)
    tall = sources * 8
    whole = received[...].astype(F32).reshape(sources * groups, 24, LANES)
    tight = groups * 8
    pitch = tight + 1
    whole = whole.reshape(sources, groups, 24, LANES)
    for source in range(sources):
        at = slice(source * pitch, source * pitch + tight)
        arrived_x[at, :] = whole[source, :, :8].reshape(tight, LANES)
        arrived_g[at, :] = whole[source, :, 8:16].reshape(tight, LANES)
    taps = whole[:, :, 16:]
    for half, holder in enumerate((taps_even, taps_odd)):
        swapped = swap_blocks([taps[:, 4 * half + q].reshape(tall, LANES) for q in range(4)])
        for one in range(4):
            for source in range(sources):
                at = (one * sources + source) * 9
                holder[at : at + 8, :] = swapped[one][source * 8 : (source + 1) * 8]

    def lanes_of(array):
        return array[:, :LANES], array[:, LANES:]

    def beside(one, two):
        return jnp.concatenate([one, two], 1)

    def wide_dot(high, low, table):
        return jnp.dot(
            jnp.concatenate([high, low, high], 1), table[...], preferred_element_type=F32
        )

    def spaced(channel, start):
        return pl.ds(channel // 4 * 8 + channel % 4 + start, sources, stride=pitch)

    def tapped(channel):
        return pl.ds(channel // 8 * (sources * 9) + channel % 8, sources, stride=9)

    def load(which, channel):
        if which == 2:
            return taps_even[tapped(channel), :], taps_odd[tapped(channel), :]
        arrived = (arrived_x, arrived_g)[which]
        return arrived[spaced(channel, 0), :], arrived[spaced(channel, 4), :]

    def store(which, channel, even, odd):
        if which == 2:
            grad_even[tapped(channel), :] = even
            grad_odd[tapped(channel), :] = odd
        else:
            leaving = (leaving_y, leaving_z)[which]
            leaving[spaced(channel, 0), :] = even
            leaving[spaced(channel, 4), :] = odd

    def enter(which, pair):
        even_one, odd_one = load(which, 2 * pair)
        even_two, odd_two = load(which, 2 * pair + 1)
        both = jnp.concatenate([beside(even_one, even_two), beside(odd_one, odd_two)], 0)
        both = both.astype(BF16)
        turned = jnp.dot(
            first[...], jnp.concatenate([both, both], 0), preferred_element_type=F32
        )
        cos, sin, masked = twist_real[...], twist_imag[...], twist_masked[...]
        for one, half in enumerate(lanes_of(turned)):
            real, imag = half[:KEPT], half[KEPT:]
            row = (2 * pair + one) * KEPT
            parts = (real * cos - imag * sin, imag * masked + real * sin)
            for part, array in enumerate(parts):
                column = slice(part * LANES, (part + 1) * LANES)
                for level, piece in enumerate(split_value(array)):
                    split[which, level, row : row + KEPT, column] = piece
                middles[which, 2 * pair + one : 2 * pair + one + 1, column] = (
                    imag[:1] * middle_twist[part : part + 1, :]
                )

    def rows_of(step):
        return slice(step * wide * KEPT, (step + 1) * wide * KEPT)

    middle_rows = slice(main, main + channels)

    def transform(which, step):
        at = rows_of(step)
        high, low = split[which, 0, at, :], split[which, 1, at, :]
        if step == 0:
            extra = split_value(middles[which])
            high = jnp.concatenate([high, extra[0]], 0)
            low = jnp.concatenate([low, extra[1]], 0)
        result = wide_dot(high, low, ahead)
        spectra[which, at, :] = result[: wide * KEPT]
        if step == 0:
            spectra[which, middle_rows, :] = result[wide * KEPT :]

    factors = ((2, 0, 1.0), (1, 2, -1.0), (1, 0, -1.0))

    def product(which, step):
        left, right, sign = factors[which]

        def part_of(index):
            whole = spectra[index, rows_of(step), :]
            if step == 0:
                whole = jnp.concatenate([whole, spectra[index, middle_rows, :]], 0)
            return lanes_of(whole)

        left_real, left_imag = part_of(left)
        right_real, right_imag = part_of(right)
        if sign > 0:
            real = left_real * right_real - left_imag * right_imag
            imag = left_imag * right_real + left_real * right_imag
        else:
            real = left_real * right_real + left_imag * right_imag
            imag = left_imag * right_real - left_real * right_imag
        turned = wide_dot(*split_value(beside(real, imag)), back)
        if step == 0:
            real, imag = lanes_of(turned[wide * KEPT :])
            cos, sin = middle_twist[:1, :], middle_twist[1:, :]
            middles[3 + which, :, :LANES] = real * cos + imag * sin
        cos, sin = twist_real[...], twist_imag[...]
        top = lax.broadcasted_iota(jnp.int32, (8, LANES), 0) == 0
        for one in range(wide):
            channel = step * wide + one
            real, imag = lanes_of(turned[one * KEPT : (one + 1) * KEPT])
            new_real = real * cos + imag * sin
            new_imag = imag * cos - real * sin
            middle = middles[3 + which, channel : channel + 1, :LANES]
            new_imag = jnp.concatenate([jnp.where(top, middle, new_imag[:8]), new_imag[8:]], 0)
            column = slice(channel % 2 * LANES, (channel % 2 + 1) * LANES)
            for part, array in enumerate((new_real, new_imag)):
                for level, piece in enumerate(split_value(array)):
                    row = (channel // 2 * 4 + 2 * level + part) * KEPT
                    weights[which, row : row + KEPT, column] = piece

    def leave(which, pair):
        signal = jnp.dot(
            last[...], weights[which, pair * 4 * KEPT : (pair + 1) * 4 * KEPT, :],
            preferred_element_type=F32,
        )
        signal = signal[: 2 * sources] + signal[2 * sources :]
        for one, half in enumerate(lanes_of(signal)):
            store(which, 2 * pair + one, half[:sources], half[sources:])

    def run(*lines):
        longest = max(len(line) for line in lines)
        for index in range(longest):
            for line in lines:
                low, high = index * len(line) // longest, (index + 1) * len(line) // longest
                for task, *where in line[low:high]:
                    task(*where)

    pairs = range(channels // 2)
    steps = range(channels // wide)

    def line(task, which):
        return [(task, which, place) for place in (pairs if task in (enter, leave) else steps)]

    run(line(enter, 0))
    run(line(enter, 1), line(transform, 0))
    run(line(enter, 2), line(transform, 1))
    run(line(transform, 2), line(product, 2))
    run(line(product, 0))
    run(line(leave, 2), line(product, 1))
    run(line(leave, 0), line(leave, 1))

    def loose(holder, first, count, size):
        starts = [(first + index) * (size + 1) for index in range(count)]
        return [holder[start : start + size, :] for start in starts]

    pieces = []
    for holder in (grad_even, grad_odd):
        swapped = swap_blocks(
            [jnp.concatenate(loose(holder, one * sources, sources, 8), 0) for one in range(4)]
        )
        pieces += [piece.reshape(sources, 8, LANES) for piece in swapped]
    grad = jnp.stack(pieces, 1).reshape(sources * groups, 8, LANES)
    made = [
        jnp.concatenate(loose(holder, 0, sources, tight), 0).reshape(sources * groups, 8, LANES)
        for holder in (leaving_y, leaving_z)
    ]
    out[...] = jnp.concatenate([*made, grad], 1).reshape(received.shape).astype(BF16)


def gather(query, key, value, cotangent, taps, ranks):
    positions, width = query.shape
    pieces = PIECES
    anywhere = pl.BlockSpec(memory_space=pl.ANY)
    return pl.pallas_call(
        gather_kernel,
        in_specs=[anywhere] * 5,
        out_specs=anywhere,
        out_shape=jax.ShapeDtypeStruct((ranks * 24, LANES), BF16),
        scratch_shapes=[
            pltpu.VMEM((pieces, 4, positions, width // pieces), BF16),
            pltpu.VMEM(taps.shape, BF16),
            pltpu.VMEM((ranks * 24, LANES), BF16),
            pltpu.SemaphoreType.DMA((pieces, 4)),
            pltpu.SemaphoreType.DMA,
            pltpu.SemaphoreType.DMA((width // LANES,)),
        ],
        compiler_params=pltpu.CompilerParams(vmem_limit_bytes=60 * MIB),
        cost_estimate=pl.CostEstimate(flops=10**6, bytes_accessed=4 * MIB, transcendentals=0),
    )(query, key, value, cotangent, taps)


def scatter(query, key, value, cotangent, back, taps_shape):
    positions, width = query.shape
    pieces = PIECES
    anywhere = pl.BlockSpec(memory_space=pl.ANY)
    return pl.pallas_call(
        scatter_kernel,
        out_specs=[anywhere] * 5,
        out_shape=[jax.ShapeDtypeStruct((positions, width), BF16)] * 4
        + [jax.ShapeDtypeStruct(taps_shape, BF16)],
        scratch_shapes=[
            pltpu.VMEM((pieces, 4, positions, width // pieces), BF16),
            pltpu.VMEM(taps_shape, BF16),
            pltpu.SemaphoreType.DMA((pieces, 4)),
            pltpu.SemaphoreType.DMA,
        ],
        compiler_params=pltpu.CompilerParams(vmem_limit_bytes=24 * MIB),
        cost_estimate=pl.CostEstimate(flops=10**6, bytes_accessed=6 * MIB, transcendentals=0),
    )(query, key, value, cotangent, back)


def long_convolution(received, seq_len):
    tables = [jnp.asarray(table) for table in make_tables(seq_len)]
    ranks = received.shape[0] // 24
    plain = pltpu.VMEM((ranks // 8 * 65 + 72, LANES), F32)
    taps = pltpu.VMEM((ranks // 2 * 9 + 16, LANES), F32)
    pair_lanes = 2 * LANES
    return pl.pallas_call(
        long_kernel,
        out_shape=jax.ShapeDtypeStruct(received.shape, BF16),
        scratch_shapes=[plain] * 4 + [taps] * 4
        + [
            pltpu.VMEM((3, 2, 32 * KEPT, pair_lanes), BF16),
            pltpu.VMEM((6, 32, pair_lanes), F32),
            pltpu.VMEM((3, 32 * KEPT + 32, pair_lanes), F32),
            pltpu.VMEM((3, 64 * KEPT, pair_lanes), BF16),
        ],
        compiler_params=pltpu.CompilerParams(vmem_limit_bytes=40 * MIB),
        cost_estimate=pl.CostEstimate(flops=10**10, bytes_accessed=3 * MIB, transcendentals=0),
    )(received, *tables)


def local(query_proj, key_proj, value_proj, cotangent, filter_taps):
    everyone = ("ctx", "tp")
    ranks = lax.axis_size("ctx") * lax.axis_size("tp")
    seq_len = query_proj.shape[0] * lax.axis_size("ctx")
    sent = gather(query_proj, key_proj, value_proj, cotangent, filter_taps, ranks)
    received = lax.all_to_all(sent, everyone, split_axis=0, concat_axis=0, tiled=True)
    made = long_convolution(received, seq_len)
    back = lax.all_to_all(made, everyone, split_axis=0, concat_axis=0, tiled=True)
    return scatter(query_proj, key_proj, value_proj, cotangent, back, filter_taps.shape)


def solution(mesh):
    placed = (P("ctx", "tp"),) * 4 + (P(("ctx", "tp"), None),)
    return jax.shard_map(local, mesh=mesh, in_specs=placed, out_specs=placed, check_vma=False)
```

```python
import functools
import math

import jax
import jax.numpy as jnp
import ml_dtypes
import numpy as np
from jax import lax
from jax.experimental import pallas as pl
from jax.experimental.pallas import tpu as pltpu
from jax.sharding import PartitionSpec as P

F32 = jnp.float32
BF16 = jnp.bfloat16
LANES = 128
KEPT = 64
MIB = 1 << 20
PIECES = 2


def split_table(table):
    high = table.astype(ml_dtypes.bfloat16)
    low = (table - high.astype(np.float64)).astype(ml_dtypes.bfloat16)
    return high, low


def make_tables(seq_len):
    radix = 2 * seq_len // LANES
    blocks = radix // 2
    total = 2 * seq_len
    order = np.concatenate([np.arange(0, blocks, 2), np.arange(1, blocks, 2)])
    k1 = np.arange(KEPT)
    turn = 2 * math.pi * np.outer(k1, order) / radix
    middle = np.cos(math.pi * order)[None]
    first = np.concatenate([np.cos(turn), middle, -np.sin(turn[1:])], 0)
    first_table = np.concatenate(split_table(first), 1)
    lane = np.arange(LANES)
    twist = 2 * math.pi * np.outer(np.arange(KEPT + 1), lane) / total
    cos, sin = np.cos(twist), -np.sin(twist)
    masked = np.where(k1[:, None] == 0, 0.0, cos[:KEPT])
    middle_twist = np.concatenate([cos[KEPT:], sin[KEPT:]], 0)
    twists = [table.astype(np.float32) for table in (cos[:KEPT], sin[:KEPT], masked, middle_twist)]
    inner = 2 * math.pi * np.outer(lane, lane) / LANES
    cos, sin = np.cos(inner), np.sin(inner)
    ahead = split_table(np.block([[cos, -sin], [sin, cos]]))
    ahead_table = np.concatenate([ahead[0], ahead[0], ahead[1]], 0)
    back = split_table(np.block([[cos, sin], [-sin, cos]]))
    back_table = np.concatenate([back[0], back[0], back[1]], 0)
    weight = np.where(k1 == 0, 1.0, 2.0)
    last = np.concatenate([np.cos(turn.T) * weight, middle.T, -2.0 * np.sin(turn[1:].T)], 1)
    high, low = split_table(last * (seq_len ** (-0.5) / total))
    last_table = np.block([[high, high], [low, np.zeros_like(low)]])
    return first_table, *twists, ahead_table, back_table, last_table


def split_value(value):
    high = value.astype(BF16)
    low = (value - high.astype(F32)).astype(BF16)
    return high, low


def swap_blocks(parts):
    block = lax.broadcasted_iota(jnp.int32, parts[0].shape, 1) // (LANES // 4)

    def exchange(parts, bit):
        upper = (block & bit) != 0
        shift = bit * (LANES // 4)
        new = list(parts)
        for low in range(4):
            if low & bit:
                continue
            high = low | bit
            new[low] = jnp.where(upper, pltpu.roll(parts[high], shift, 1), parts[low])
            new[high] = jnp.where(upper, parts[high], pltpu.roll(parts[low], LANES - shift, 1))
        return new

    return exchange(exchange(parts, 2), 1)


def pair_rows(left, right):
    low = lax.broadcasted_iota(jnp.int32, left.shape, 1) < 4
    return (
        jnp.where(low, left, pltpu.roll(right, 4, 1)),
        jnp.where(low, pltpu.roll(left, 4, 1), right),
    )


def gather_kernel(
    query, key, value, cotangent, taps, out, wide, taps_here, out_here, sems, taps_sem, out_sems
):
    pieces, _, _, width = wide.shape
    channels = taps.shape[1]
    parts = width // LANES
    rows = out.shape[0] // pieces // parts

    def columns(piece):
        return pl.ds(piece * width, width)

    loads = [
        [
            pltpu.make_async_copy(
                array.at[:, columns(piece)], wide.at[piece, index], sems.at[piece, index]
            )
            for index, array in enumerate((key, value, cotangent, query))
        ]
        for piece in range(pieces)
    ]
    taps_load = pltpu.make_async_copy(taps, taps_here, taps_sem)
    stores = [
        pltpu.make_async_copy(
            out_here.at[pl.ds(block * rows, rows)],
            out.at[pl.ds(block * rows, rows)],
            out_sems.at[block],
        )
        for block in range(pieces * parts)
    ]
    for piece in range(pieces):
        for load in loads[piece]:
            load.start()
        if piece == 0:
            taps_load.start()

    def interleave(left, right):
        left, right = pair_rows(left.reshape(-1, 8, LANES), right.reshape(-1, 8, LANES))
        return jnp.stack([left, right], 1).reshape(-1, 8, LANES)

    def turn(left, right):
        turned = (left.astype(F32) * right.astype(F32)).astype(BF16).T.astype(F32)
        return interleave(turned[:, :LANES], turned[:, LANES:])

    def turn_taps(start):
        def some(first):
            parts = []
            for tp in range(first, 8, 2):
                at = tp * (channels // 8) + start
                parts.append(taps_here[:, at : at + LANES])
            return jnp.concatenate(parts, 0).T.astype(F32)

        return interleave(some(0), some(1))

    for piece in range(pieces):
        for load in loads[piece]:
            load.wait()
        if piece == 0:
            taps_load.wait()
        for part in range(parts):
            column = slice(part * LANES, (part + 1) * LANES)
            whole = jnp.concatenate(
                [
                    turn(wide[piece, 0, :, column], wide[piece, 1, :, column]),
                    turn(wide[piece, 2, :, column], wide[piece, 3, :, column]),
                    turn_taps(piece * width + part * LANES),
                ],
                1,
            )
            block = piece * parts + part
            out_here[block * rows : (block + 1) * rows, :] = whole.reshape(rows, LANES).astype(BF16)
            stores[block].start()
    for store in stores:
        store.wait()


def scatter_kernel(
    query, key, value, cotangent, back,
    block_output, grad_query, grad_key, grad_value, grad_filter,
    wide, taps_here, sems, taps_sem,
):
    pieces, _, _, width = wide.shape
    tap_rows, channels = grad_filter.shape
    rows = LANES // 4 * 24
    stores = [
        [
            pltpu.make_async_copy(
                wide.at[piece, index],
                array.at[:, pl.ds(piece * width, width)],
                sems.at[piece, index],
            )
            for index, array in enumerate((block_output, grad_query, grad_key, grad_value))
        ]
        for piece in range(pieces)
    ]
    taps_store = pltpu.make_async_copy(taps_here, grad_filter, taps_sem)

    def separate(array):
        array = array.reshape(-1, 2, 8, LANES)
        left, right = pair_rows(array[:, 0], array[:, 1])
        return left.reshape(-1, LANES), right.reshape(-1, LANES)

    def turn(array):
        return jnp.concatenate(separate(array), 1).astype(BF16).T.astype(F32)

    def arrived(block):
        return back[block * rows : (block + 1) * rows, :].astype(F32).reshape(-1, 24, LANES)

    for block in range(pieces * width // LANES):
        for first, taps in enumerate(separate(arrived(block)[:, 16:])):
            turned = taps.astype(BF16).T
            for one in range(4):
                at = (2 * one + first) * (channels // 8) + block * LANES
                taps_here[:, at : at + LANES] = turned[one * tap_rows : (one + 1) * tap_rows]
    taps_store.start()
    for piece in range(pieces):
        for start, factors in ((0, (query, cotangent)), (8, (value, key))):
            for part in range(width // LANES):
                block = piece * (width // LANES) + part
                column = slice(block * LANES, (block + 1) * LANES)
                signal = turn(arrived(block)[:, start : start + 8])
                for index, factor in enumerate(factors):
                    product = (factor[:, column].astype(F32) * signal).astype(BF16)
                    wide[piece, start // 4 + index, :, part * LANES : (part + 1) * LANES] = product
            for index in range(2):
                stores[piece][start // 4 + index].start()
    for piece in range(pieces):
        for store in stores[piece]:
            store.wait()
    taps_store.wait()


def long_kernel(
    received, first, twist_real, twist_imag, twist_masked, middle_twist, ahead, back, last, out,
    arrived_x, arrived_g, leaving_y, leaving_z, taps_even, taps_odd, grad_even, grad_odd, split, middles, spectra, weights,
):
    groups = 8
    channels = 32
    wide = 8
    main = channels * KEPT
    sources = received.shape[0] // (groups * 24)
    tall = sources * 8
    whole = received[...].astype(F32).reshape(sources * groups, 24, LANES)
    tight = groups * 8
    pitch = tight + 1
    whole = whole.reshape(sources, groups, 24, LANES)
    for source in range(sources):
        at = slice(source * pitch, source * pitch + tight)
        arrived_x[at, :] = whole[source, :, :8].reshape(tight, LANES)
        arrived_g[at, :] = whole[source, :, 8:16].reshape(tight, LANES)
    taps = whole[:, :, 16:]
    for half, holder in enumerate((taps_even, taps_odd)):
        swapped = swap_blocks([taps[:, 4 * half + q].reshape(tall, LANES) for q in range(4)])
        for one in range(4):
            for source in range(sources):
                at = (one * sources + source) * 9
                holder[at : at + 8, :] = swapped[one][source * 8 : (source + 1) * 8]

    def lanes_of(array):
        return array[:, :LANES], array[:, LANES:]

    def beside(one, two):
        return jnp.concatenate([one, two], 1)

    def wide_dot(high, low, table):
        return jnp.dot(
            jnp.concatenate([high, low, high], 1), table[...], preferred_element_type=F32
        )

    def spaced(channel, start):
        return pl.ds(channel // 4 * 8 + channel % 4 + start, sources, stride=pitch)

    def tapped(channel):
        return pl.ds(channel // 8 * (sources * 9) + channel % 8, sources, stride=9)

    def load(which, channel):
        if which == 2:
            return taps_even[tapped(channel), :], taps_odd[tapped(channel), :]
        arrived = (arrived_x, arrived_g)[which]
        return arrived[spaced(channel, 0), :], arrived[spaced(channel, 4), :]

    def store(which, channel, even, odd):
        if which == 2:
            grad_even[tapped(channel), :] = even
            grad_odd[tapped(channel), :] = odd
        else:
            leaving = (leaving_y, leaving_z)[which]
            leaving[spaced(channel, 0), :] = even
            leaving[spaced(channel, 4), :] = odd

    def enter(which, pair):
        even_one, odd_one = load(which, 2 * pair)
        even_two, odd_two = load(which, 2 * pair + 1)
        both = jnp.concatenate([beside(even_one, even_two), beside(odd_one, odd_two)], 0)
        both = both.astype(BF16)
        turned = jnp.dot(
            first[...], jnp.concatenate([both, both], 0), preferred_element_type=F32
        )
        cos, sin, masked = twist_real[...], twist_imag[...], twist_masked[...]
        for one, half in enumerate(lanes_of(turned)):
            real, imag = half[:KEPT], half[KEPT:]
            row = (2 * pair + one) * KEPT
            parts = (real * cos - imag * sin, imag * masked + real * sin)
            for part, array in enumerate(parts):
                column = slice(part * LANES, (part + 1) * LANES)
                for level, piece in enumerate(split_value(array)):
                    split[which, level, row : row + KEPT, column] = piece
                middles[which, 2 * pair + one : 2 * pair + one + 1, column] = (
                    imag[:1] * middle_twist[part : part + 1, :]
                )

    def rows_of(step):
        return slice(step * wide * KEPT, (step + 1) * wide * KEPT)

    middle_rows = slice(main, main + channels)

    def transform(which, step):
        at = rows_of(step)
        high, low = split[which, 0, at, :], split[which, 1, at, :]
        if step == 0:
            extra = split_value(middles[which])
            high = jnp.concatenate([high, extra[0]], 0)
            low = jnp.concatenate([low, extra[1]], 0)
        result = wide_dot(high, low, ahead)
        spectra[which, at, :] = result[: wide * KEPT]
        if step == 0:
            spectra[which, middle_rows, :] = result[wide * KEPT :]

    factors = ((2, 0, 1.0), (1, 2, -1.0), (1, 0, -1.0))

    def product(which, step):
        left, right, sign = factors[which]

        def part_of(index):
            whole = spectra[index, rows_of(step), :]
            if step == 0:
                whole = jnp.concatenate([whole, spectra[index, middle_rows, :]], 0)
            return lanes_of(whole)

        left_real, left_imag = part_of(left)
        right_real, right_imag = part_of(right)
        if sign > 0:
            real = left_real * right_real - left_imag * right_imag
            imag = left_imag * right_real + left_real * right_imag
        else:
            real = left_real * right_real + left_imag * right_imag
            imag = left_imag * right_real - left_real * right_imag
        turned = wide_dot(*split_value(beside(real, imag)), back)
        if step == 0:
            real, imag = lanes_of(turned[wide * KEPT :])
            cos, sin = middle_twist[:1, :], middle_twist[1:, :]
            middles[3 + which, :, :LANES] = real * cos + imag * sin
        cos, sin = twist_real[...], twist_imag[...]
        top = lax.broadcasted_iota(jnp.int32, (8, LANES), 0) == 0
        for one in range(wide):
            channel = step * wide + one
            real, imag = lanes_of(turned[one * KEPT : (one + 1) * KEPT])
            new_real = real * cos + imag * sin
            new_imag = imag * cos - real * sin
            middle = middles[3 + which, channel : channel + 1, :LANES]
            new_imag = jnp.concatenate([jnp.where(top, middle, new_imag[:8]), new_imag[8:]], 0)
            column = slice(channel % 2 * LANES, (channel % 2 + 1) * LANES)
            for part, array in enumerate((new_real, new_imag)):
                for level, piece in enumerate(split_value(array)):
                    row = (channel // 2 * 4 + 2 * level + part) * KEPT
                    weights[which, row : row + KEPT, column] = piece

    def leave(which, pair):
        signal = jnp.dot(
            last[...], weights[which, pair * 4 * KEPT : (pair + 1) * 4 * KEPT, :],
            preferred_element_type=F32,
        )
        signal = signal[: 2 * sources] + signal[2 * sources :]
        for one, half in enumerate(lanes_of(signal)):
            store(which, 2 * pair + one, half[:sources], half[sources:])

    def run(*lines):
        longest = max(len(line) for line in lines)
        for index in range(longest):
            for line in lines:
                low, high = index * len(line) // longest, (index + 1) * len(line) // longest
                for task, *where in line[low:high]:
                    task(*where)

    pairs = range(channels // 2)
    steps = range(channels // wide)

    def line(task, which):
        return [(task, which, place) for place in (pairs if task in (enter, leave) else steps)]

    run(line(enter, 0))
    run(line(enter, 1), line(transform, 0))
    run(line(enter, 2), line(transform, 1))
    run(line(transform, 2), line(product, 2))
    run(line(product, 0))
    run(line(leave, 2), line(product, 1))
    run(line(leave, 0), line(leave, 1))

    def loose(holder, first, count, size):
        starts = [(first + index) * (size + 1) for index in range(count)]
        return [holder[start : start + size, :] for start in starts]

    pieces = []
    for holder in (grad_even, grad_odd):
        swapped = swap_blocks(
            [jnp.concatenate(loose(holder, one * sources, sources, 8), 0) for one in range(4)]
        )
        pieces += [piece.reshape(sources, 8, LANES) for piece in swapped]
    grad = jnp.stack(pieces, 1).reshape(sources * groups, 8, LANES)
    made = [
        jnp.concatenate(loose(holder, 0, sources, tight), 0).reshape(sources * groups, 8, LANES)
        for holder in (leaving_y, leaving_z)
    ]
    out[...] = jnp.concatenate([*made, grad], 1).reshape(received.shape).astype(BF16)


def gather(query, key, value, cotangent, taps, ranks):
    positions, width = query.shape
    pieces = PIECES
    anywhere = pl.BlockSpec(memory_space=pl.ANY)
    return pl.pallas_call(
        gather_kernel,
        in_specs=[anywhere] * 5,
        out_specs=anywhere,
        out_shape=jax.ShapeDtypeStruct((ranks * 24, LANES), BF16),
        scratch_shapes=[
            pltpu.VMEM((pieces, 4, positions, width // pieces), BF16),
            pltpu.VMEM(taps.shape, BF16),
            pltpu.VMEM((ranks * 24, LANES), BF16),
            pltpu.SemaphoreType.DMA((pieces, 4)),
            pltpu.SemaphoreType.DMA,
            pltpu.SemaphoreType.DMA((width // LANES,)),
        ],
        compiler_params=pltpu.CompilerParams(vmem_limit_bytes=60 * MIB),
        cost_estimate=pl.CostEstimate(flops=10**6, bytes_accessed=4 * MIB, transcendentals=0),
    )(query, key, value, cotangent, taps)


def scatter(query, key, value, cotangent, back, taps_shape):
    positions, width = query.shape
    pieces = 2 * PIECES
    anywhere = pl.BlockSpec(memory_space=pl.ANY)
    return pl.pallas_call(
        scatter_kernel,
        out_specs=[anywhere] * 5,
        out_shape=[jax.ShapeDtypeStruct((positions, width), BF16)] * 4
        + [jax.ShapeDtypeStruct(taps_shape, BF16)],
        scratch_shapes=[
            pltpu.VMEM((pieces, 4, positions, width // pieces), BF16),
            pltpu.VMEM(taps_shape, BF16),
            pltpu.SemaphoreType.DMA((pieces, 4)),
            pltpu.SemaphoreType.DMA,
        ],
        compiler_params=pltpu.CompilerParams(vmem_limit_bytes=24 * MIB),
        cost_estimate=pl.CostEstimate(flops=10**6, bytes_accessed=6 * MIB, transcendentals=0),
    )(query, key, value, cotangent, back)


def long_convolution(received, seq_len):
    tables = [jnp.asarray(table) for table in make_tables(seq_len)]
    ranks = received.shape[0] // 24
    plain = pltpu.VMEM((ranks // 8 * 65 + 72, LANES), F32)
    taps = pltpu.VMEM((ranks // 2 * 9 + 16, LANES), F32)
    pair_lanes = 2 * LANES
    return pl.pallas_call(
        long_kernel,
        out_shape=jax.ShapeDtypeStruct(received.shape, BF16),
        scratch_shapes=[plain] * 4 + [taps] * 4
        + [
            pltpu.VMEM((3, 2, 32 * KEPT, pair_lanes), BF16),
            pltpu.VMEM((6, 32, pair_lanes), F32),
            pltpu.VMEM((3, 32 * KEPT + 32, pair_lanes), F32),
            pltpu.VMEM((3, 64 * KEPT, pair_lanes), BF16),
        ],
        compiler_params=pltpu.CompilerParams(vmem_limit_bytes=40 * MIB),
        cost_estimate=pl.CostEstimate(flops=10**10, bytes_accessed=3 * MIB, transcendentals=0),
    )(received, *tables)


def local(query_proj, key_proj, value_proj, cotangent, filter_taps):
    everyone = ("ctx", "tp")
    ranks = lax.axis_size("ctx") * lax.axis_size("tp")
    seq_len = query_proj.shape[0] * lax.axis_size("ctx")
    sent = gather(query_proj, key_proj, value_proj, cotangent, filter_taps, ranks)
    received = lax.all_to_all(sent, everyone, split_axis=0, concat_axis=0, tiled=True)
    made = long_convolution(received, seq_len)
    back = lax.all_to_all(made, everyone, split_axis=0, concat_axis=0, tiled=True)
    return scatter(query_proj, key_proj, value_proj, cotangent, back, filter_taps.shape)


def solution(mesh):
    placed = (P("ctx", "tp"),) * 4 + (P(("ctx", "tp"), None),)
    return jax.shard_map(local, mesh=mesh, in_specs=placed, out_specs=placed, check_vma=False)
```
